32 devices in a mesh: dp: 4 (over z), seq: 8 (over y, x, core).
Axes of the slice: x: 2, y: 2, z: 4, core: 2. Of those that a mesh axis runs over, the one named last changes fastest.
Arguments:
- tokens: int32 [1024, 16], P('seq', 'dp'), may hold values from 0 to 31999
- segments: int32 [1024, 16], P('seq', 'dp'), may hold values from 0 to 1, as said below
- masked_pick: int32 [608, 4], P('seq', 'dp'), may hold values from 0 to 511
- masked_labels: int32 [608, 4], replicated, may hold values from -1 to 31999, as said below
- pair_labels: int32 [16], P('dp'), may hold values from 0 to 1
- embedding: float32 [32000, 768], P('seq')
- embed_first: float32 [32000, 768], P('seq'), may hold values from -0.0024414062 to 0.0024414062
- embed_second: float32 [32000, 768], P('seq'), may hold values from 2.8216196e-08 to 1.1286478e-07
- position_table: float32 [1024, 768], P('seq'), may hold values from -0.4375 to 0.4375
- position_first: float32 [1024, 768], P('seq'), may hold values from -0.0024414062 to 0.0024414062
- position_second: float32 [1024, 768], P('seq'), may hold values from 2.8216196e-08 to 1.1286478e-07
- head_bias: float32 [32000], P('seq'), may hold values from -3 to 3
- head_first: float32 [32000], P('seq'), may hold values from -0.009765625 to 0.009765625
- head_second: float32 [32000], P('seq'), may hold values from 4.5145913e-07 to 1.8058365e-06
- vectors: float32 [17, 768], replicated
- vector_first: float32 [17, 768], replicated, may hold values from -0.009765625 to 0.009765625
- vector_second: float32 [17, 768], replicated, may hold values from 4.5145913e-07 to 1.8058365e-06
- inner_bias: float32 [2, 3072], replicated, may hold values from -1.5 to 1.5
- inner_first: float32 [2, 3072], replicated, may hold values from -0.0024414062 to 0.0024414062
- inner_second: float32 [2, 3072], replicated, may hold values from 2.8216196e-08 to 1.1286478e-07
- pooler: float32 [768, 768], replicated, may hold values from -0.21875 to 0.21875
- pooler_first: float32 [768, 768], replicated, may hold values from -0.0024414062 to 0.0024414062
- pooler_second: float32 [768, 768], replicated, may hold values from 2.8216196e-08 to 1.1286478e-07
- feed_weights: float32 [768, 12288], P(None, ('dp', 'seq'))
- feed_moment: float32 [768, 12288], P(None, ('dp', 'seq')), may hold values from -0.0024414062 to 0.0024414062
Outputs:
- loss: float32 [], replicated
- masked_count: float32 [], replicated
- grad_norm: float32 [], replicated
- new_embedding: float32 [32000, 768], P('seq')
- new_embed_first: float32 [32000, 768], P('seq')
- new_embed_second: float32 [32000, 768], P('seq')
- new_position_table: float32 [1024, 768], P('seq')
- new_position_first: float32 [1024, 768], P('seq')
- new_position_second: float32 [1024, 768], P('seq')
- new_head_bias: float32 [32000], P('seq')
- new_head_first: float32 [32000], P('seq')
- new_head_second: float32 [32000], P('seq')
- new_vectors: float32 [17, 768], replicated
- new_vector_first: float32 [17, 768], replicated
- new_vector_second: float32 [17, 768], replicated
- new_inner_bias: float32 [2, 3072], replicated
- new_inner_first: float32 [2, 3072], replicated
- new_inner_second: float32 [2, 3072], replicated
- new_pooler: float32 [768, 768], replicated
- new_pooler_first: float32 [768, 768], replicated
- new_pooler_second: float32 [768, 768], replicated
- new_feed_weights: float32 [768, 12288], P(None, ('dp', 'seq'))
- new_feed_moment: float32 [768, 12288], P(None, ('dp', 'seq'))
The draws below stay inside these ranges and needn't reach their ends.
Inputs may be any that keep to these rules, and one draw needn't show every extreme that they name: `segments`: along each item's positions the ids are 0 and then 1, each at least once. `masked_labels`: row r belongs to position block r // 76, column g to item group g; -1 marks an unused slot.
All inputs are finite; a program needn't handle non-finite values.
Results may differ from the reference program's by a relative error of at most 0.015.
Values may be sent and summed in bfloat16 or wider, within the bound.
No kernel may reach another device: no remote copies, remote signals or barrier semaphores. Data moves between devices by JAX's collectives and lax.ppermute only.
A program may use at most 320 MiB of HBM per device.

```python
import math
import jax
import jax.numpy as jnp
import numpy as np
from jax import lax

D = 768
FF = 3072
V = 32000
NL = 2
ITEMS_G = 4
STEP = 10
SEQ_LEN = 1024
BLK = 128
ITEMS = 16
MSK = 76
MATS = 4
NVEC = 17
PARAMS = 35440640
N_DP = 4
N_SEQ = 8


def draw_segments(key, part):
    key = jax.random.fold_in(key, 1)
    bounds = jax.random.randint(key, (ITEMS,), 1, SEQ_LEN)
    places = jnp.arange(SEQ_LEN, dtype=jnp.int32)[:, None]
    return (places >= bounds[None, :]).astype(jnp.int32)


def draw_masked_labels(key, part):
    key = jax.random.fold_in(key, 2)
    chance_key, label_key = jax.random.split(key)
    shape = (N_SEQ * MSK, N_DP)
    spread = max(N_SEQ - 1, 1)
    block_of = (jnp.arange(N_SEQ * MSK, dtype=jnp.int32) // MSK)[:, None]
    chance = jax.random.randint(chance_key, shape, 0, 3 * spread)
    labels = jax.random.randint(label_key, shape, 0, V)
    return jnp.where(chance < spread + 2 * block_of, labels, -1)


def draw_embedding(key, part):
    key = jax.random.fold_in(key, 3)
    place = jnp.arange(V, dtype=jnp.float32)[:, None] / V
    base = jax.random.normal(key, (V, D), jnp.float32)
    rising = 1.0 + 2.0 * place
    return base * rising / math.sqrt(D)


def draw_vectors(key, part):
    key = jax.random.fold_in(key, 4)
    norms = 2 * NL + 1
    index = jnp.arange(NVEC, dtype=jnp.int32)[:, None]
    base = jax.random.normal(key, (NVEC, D), jnp.float32)
    is_gain = (index >= 2) & (index < 2 + norms)
    is_class = index >= NVEC - 2
    spread = jnp.where(index < 2, 0.02, jnp.where(is_gain, 0.1, jnp.where(is_class, 1.0 / math.sqrt(D), 0.1)))
    return jnp.where(is_gain, 1.0, 0.0) + spread * base


def draw_feed_weights(key, part):
    key = jax.random.fold_in(key, 5)
    column = jnp.arange(MATS * FF, dtype=jnp.int32)
    within = (column % FF).astype(jnp.float32) / FF
    fan = jnp.where(column // FF % 2 == 0, float(D), float(FF))
    base = jax.random.normal(key, (D, MATS * FF), jnp.float32)
    rising = (1.0 + 2.0 * within) / math.sqrt(13.0 / 3.0)
    return base * (rising / jnp.sqrt(fan))[None, :]


def place_ends(values, rng, least, largest):
    longest = values.shape.index(max(values.shape))
    spots = []
    for shift in (0, 1):
        where = [jax.random.randint(jax.random.fold_in(rng, axis), (), 0, length) for axis, length in enumerate(values.shape)]
        where[longest] = (where[longest] + shift) % values.shape[longest]
        spots.append(tuple(where))
    return values.at[spots[0]].set(least).at[spots[1]].set(largest)


def block_scale(key, dims, cuts, smallest, high):
    gain, own = 1.0, jax.random.fold_in(key, 6)
    for position, blocks in cuts:
        steps = jnp.exp(jax.random.uniform(jax.random.fold_in(own, position), (blocks,), jnp.float32, smallest / len(cuts), high / len(cuts)))
        gain = gain * jnp.repeat(steps, dims[position] // blocks).reshape([-1 if axis == position else 1 for axis in range(len(dims))])
    return gain


def rank_bounds(count, slope):
    loads = [(1 << 20) // math.isqrt(standing ** slope) + 1 for standing in range(1, count + 1)]
    deviation = 1 + sum(loads) // (1 << 30)
    return np.cumsum(np.array([max(1, weight // deviation) for weight in loads]))


def skewed_ids(rng, dims, amount, slope):
    grid = rank_bounds(amount, slope)
    pick = jax.random.randint(jax.random.fold_in(rng, 1), dims, 0, int(grid[amount - 1]))
    standing = jnp.searchsorted(jnp.asarray(grid, jnp.int32), pick, side="right")
    return jax.random.permutation(jax.random.fold_in(rng, 2), amount)[standing].astype(jnp.int32)


def bell_draw(stream_key, dims, deviation, reach, cuts=(), kind=jnp.bfloat16):
    drawn = jax.random.normal(stream_key, dims, jnp.float32) * deviation
    if len(cuts) > 0:
        drawn = block_scale(stream_key, dims, cuts, -0.22, 0.18) * drawn
    return jnp.clip(drawn, min=-reach, max=reach).astype(kind)


def setup_inputs(seed: int = 0) -> dict:
    keys = jax.random.split(jax.random.key(seed), 26)
    return {
        "tokens": place_ends(skewed_ids(keys[0], (SEQ_LEN, ITEMS), V, 2), jax.random.fold_in(keys[0], 3), 0, V - 1).astype(jnp.int32),
        "segments": draw_segments(jax.random.fold_in(keys[25], 71), 0),
        "masked_pick": place_ends(jax.random.randint(keys[2], (N_SEQ * MSK, N_DP), 0, BLK * ITEMS_G), jax.random.fold_in(keys[2], 1), 0, (BLK * ITEMS_G) - 1).astype(jnp.int32),
        "masked_labels": draw_masked_labels(jax.random.fold_in(keys[25], 71), 0),
        "pair_labels": place_ends(jax.random.randint(keys[4], (ITEMS,), 0, 2), jax.random.fold_in(keys[4], 1), 0, 1).astype(jnp.int32),
        "embedding": draw_embedding(jax.random.fold_in(keys[25], 71), 0),
        "embed_first": bell_draw(keys[6], (V, D), (PARAMS ** -0.5), 0.0024414062, ((0, 8),), jnp.float32),
        "embed_second": jnp.clip(jnp.exp(math.log(1.1286478240890574e-07) - 1.3862944 * jax.random.uniform(keys[7], (V, D), jnp.float32) ** block_scale(keys[7], (V, D), ((0, 8),), -0.2, 0.2)), 2.8216195602226435e-08, 1.1286478240890574e-07),
        "position_table": bell_draw(keys[8], (SEQ_LEN, D), 0.03, 0.4375, ((0, 8),), jnp.float32),
        "position_first": bell_draw(keys[9], (SEQ_LEN, D), (PARAMS ** -0.5), 0.0024414062, ((0, 8),), jnp.float32),
        "position_second": jnp.clip(jnp.exp(math.log(1.1286478240890574e-07) - 1.3862944 * jax.random.uniform(keys[10], (SEQ_LEN, D), jnp.float32) ** block_scale(keys[10], (SEQ_LEN, D), ((0, 8),), -0.2, 0.2)), 2.8216195602226435e-08, 1.1286478240890574e-07),
        "head_bias": bell_draw(keys[11], (V,), 0.5, 3.0, ((0, 8),), jnp.float32),
        "head_first": bell_draw(keys[12], (V,), (4 * PARAMS ** -0.5), 0.009765625, ((0, 8),), jnp.float32),
        "head_second": jnp.clip(jnp.exp(math.log(1.8058365185424918e-06) - 1.3862944 * jax.random.uniform(keys[13], (V,), jnp.float32) ** block_scale(keys[13], (V,), ((0, 8),), -0.2, 0.2)), 4.5145912963562296e-07, 1.8058365185424918e-06),
        "vectors": draw_vectors(jax.random.fold_in(keys[25], 71), 0),
        "vector_first": bell_draw(keys[15], (NVEC, D), (4 * PARAMS ** -0.5), 0.009765625, (), jnp.float32),
        "vector_second": jnp.clip(jnp.exp(jax.random.uniform(keys[16], (NVEC, D), jnp.float32, math.log(4.5145912963562296e-07), math.log(1.8058365185424918e-06))), 4.5145912963562296e-07, 1.8058365185424918e-06),
        "inner_bias": bell_draw(keys[17], (NL, FF), 0.1, 1.5, (), jnp.float32),
        "inner_first": bell_draw(keys[18], (NL, FF), (PARAMS ** -0.5), 0.0024414062, (), jnp.float32),
        "inner_second": jnp.clip(jnp.exp(jax.random.uniform(keys[19], (NL, FF), jnp.float32, math.log(2.8216195602226435e-08), math.log(1.1286478240890574e-07))), 2.8216195602226435e-08, 1.1286478240890574e-07),
        "pooler": bell_draw(keys[20], (D, D), D ** -0.5, 0.21875, (), jnp.float32),
        "pooler_first": bell_draw(keys[21], (D, D), (PARAMS ** -0.5), 0.0024414062, (), jnp.float32),
        "pooler_second": jnp.clip(jnp.exp(jax.random.uniform(keys[22], (D, D), jnp.float32, math.log(2.8216195602226435e-08), math.log(1.1286478240890574e-07))), 2.8216195602226435e-08, 1.1286478240890574e-07),
        "feed_weights": draw_feed_weights(jax.random.fold_in(keys[25], 71), 0),
        "feed_moment": bell_draw(keys[24], (D, MATS * FF), (PARAMS ** -0.5), 0.0024414062, ((1, 32),), jnp.float32),
    }


@jax.custom_vjp
def low(v):
    return lax.optimization_barrier(v.astype(jnp.bfloat16)).astype(jnp.float32)

@jax.custom_vjp
def low_back(v):
    return v

def low_keep(v):
    return (low(v), None)

def low_pass(kept, grad):
    return (grad,)

def back_keep(v):
    return (v, None)

def back_low(kept, grad):
    return (low(grad),)
low.defvjp(low_keep, low_pass)
low_back.defvjp(back_keep, back_low)
highest = lax.Precision.HIGHEST
norm_epsilon = 1e-06
beta_one = 0.5
beta_two = 0.5
adam_epsilon = 1e-08
decay = 0.01
clip_limit = 1.0
muon_rate = 0.05
muon_keep = 0.5
ns_first = 3.4445
ns_second = -4.775
ns_third = 2.0315

def vector_rates(layers):
    rates = [0.01, 0.01] + [0.2] * (2 * layers + 1) + [0.05] * (2 * layers + 1) + [0.05] * layers + [0.05, 0.02, 0.02]
    return jnp.array(rates, jnp.float32)[:, None]

def dft_table(first_row, row_total, length):
    rows_idx = first_row + jnp.arange(row_total, dtype=jnp.int32)
    cols_idx = jnp.arange(length, dtype=jnp.int32)
    phase = rows_idx[:, None] * cols_idx[None, :] % length
    angle = phase.astype(jnp.float32) * (2.0 * math.pi / length)
    return (jnp.cos(angle), jnp.sin(angle))

def layer_norm(values, scales, shifts):
    average = lax.optimization_barrier(jnp.mean(values, axis=-1, keepdims=True))
    centred = values - average
    variance = lax.optimization_barrier(jnp.mean(centred * centred, axis=-1, keepdims=True))
    return centred * lax.rsqrt(variance + norm_epsilon) * scales + shifts

def pair_loss(first_tokens, pool_weight, pool_shift, class_rows, labels_pair):
    pooled = jnp.tanh(jnp.dot(first_tokens, pool_weight, precision=highest) + pool_shift)
    scores = jnp.dot(pooled, class_rows.T, precision=highest)
    peak = lax.optimization_barrier(jnp.max(scores, axis=1, keepdims=True))
    log_total = peak[:, 0] + jnp.log(lax.optimization_barrier(jnp.sum(jnp.exp(scores - peak), axis=1)))
    chosen = jnp.take_along_axis(scores, labels_pair[:, None], axis=1)[:, 0]
    return jnp.sum(log_total - chosen)

def forward(embedding, position_table, head_bias, vectors, inner_bias, pooler, feed_weights, tokens, segments, masked_pick, masked_labels, pair_labels):
    seq_length, items = tokens.shape
    width = embedding.shape[1]
    layers, hidden = inner_bias.shape
    norms = 2 * layers + 1
    emb_low = low(embedding)
    feed_low = low(feed_weights)
    cos_hid, sin_hid = [low(table) for table in dft_table(0, width, width)]
    cos_seq, sin_seq = [low(table) for table in dft_table(0, seq_length, seq_length)]
    embedded = low_back(emb_low[tokens])
    sentence = jnp.where(segments[..., None] == 1, vectors[1], vectors[0])
    stream = layer_norm(embedded + position_table[:, None, :] + sentence, vectors[2], vectors[2 + norms])
    for layer_index in range(layers):
        stream_low = low(stream)
        part_a = low_back(low(jnp.dot(stream_low, cos_hid, precision=highest)))
        part_b = low_back(low(jnp.dot(stream_low, sin_hid, precision=highest)))
        mixed = jnp.dot(cos_seq, part_a.reshape(seq_length, -1), precision=highest) - jnp.dot(sin_seq, part_b.reshape(seq_length, -1), precision=highest)
        mixed = low_back(low(mixed.reshape(stream.shape)))
        joined = layer_norm(stream + mixed, vectors[3 + 2 * layer_index], vectors[3 + 2 * layer_index + norms])
        w_in = feed_low[:, 2 * layer_index * hidden:(2 * layer_index + 1) * hidden]
        w_out = feed_low[:, (2 * layer_index + 1) * hidden:(2 * layer_index + 2) * hidden]
        inner = low_back(jnp.dot(low(joined), w_in, precision=highest)) + inner_bias[layer_index]
        active = low(jax.nn.gelu(inner, approximate=True))
        output = low_back(jnp.einsum('lbf,df->lbd', active, w_out, precision=highest)) + vectors[2 + 2 * norms + layer_index]
        stream = layer_norm(joined + output, vectors[4 + 2 * layer_index], vectors[4 + 2 * layer_index + norms])
    flattened = stream.reshape(seq_length * items, width)
    block_of = jnp.arange(masked_pick.shape[0], dtype=jnp.int32)[:, None] // MSK
    group_of = jnp.arange(masked_pick.shape[1], dtype=jnp.int32)[None, :]
    place = block_of * BLK + masked_pick // ITEMS_G
    member = group_of * ITEMS_G + masked_pick % ITEMS_G
    index = (place * items + member).T
    masked_rows = flattened[index]
    labels_t = masked_labels.T
    masked_count = jnp.sum(labels_t >= 0).astype(jnp.float32)

    def head_block(pair):
        rows_group, labels_group = pair
        logits = low_back(jnp.dot(low(rows_group), emb_low.T, precision=highest)) + head_bias
        peak = lax.optimization_barrier(jnp.max(logits, axis=1, keepdims=True))
        log_total = peak[:, 0] + jnp.log(lax.optimization_barrier(jnp.sum(jnp.exp(logits - peak), axis=1)))
        target = jnp.take_along_axis(logits, jnp.maximum(labels_group, 0)[:, None], axis=1)[:, 0]
        return jnp.sum(jnp.where(labels_group >= 0, log_total - target, 0.0))
    masked_sum = jnp.sum(lax.map(jax.checkpoint(head_block), (masked_rows, labels_t)))
    pool_row = 2 + 2 * norms + layers
    pair_sum = pair_loss(stream[0], pooler, vectors[pool_row], vectors[pool_row + 1:pool_row + 3], pair_labels)
    loss = masked_sum / masked_count + pair_sum / items
    return (loss, masked_count)

def adam_step(weight, grad, first, second, rate):
    first = beta_one * first + (1.0 - beta_one) * grad
    second = beta_two * second + (1.0 - beta_two) * grad * grad
    first_hat = first / (1.0 - beta_one ** STEP)
    second_hat = second / (1.0 - beta_two ** STEP)
    weight = weight - rate * (first_hat / (jnp.sqrt(second_hat) + adam_epsilon) + decay * weight)
    return (weight, first, second)

def reference(tokens, segments, masked_pick, masked_labels, pair_labels, embedding, embed_first, embed_second, position_table, position_first, position_second, head_bias, head_first, head_second, vectors, vector_first, vector_second, inner_bias, inner_first, inner_second, pooler, pooler_first, pooler_second, feed_weights, feed_moment):

    def loss_of(*weights):
        return forward(*weights, tokens, segments, masked_pick, masked_labels, pair_labels)
    weights = (embedding, position_table, head_bias, vectors, inner_bias, pooler, feed_weights)
    loss, pullback, masked_count = jax.vjp(loss_of, *weights, has_aux=True)
    grads = pullback(jnp.ones_like(loss))
    squares = sum((jnp.sum(grad * grad) for grad in grads))
    grad_norm = jnp.sqrt(squares)
    clip = clip_limit / jnp.maximum(grad_norm, clip_limit)
    grads = [grad * clip for grad in grads]
    layers, hidden = inner_bias.shape
    width = embedding.shape[1]
    new_emb = adam_step(embedding, grads[0], embed_first, embed_second, 0.02)
    new_pos = adam_step(position_table, grads[1], position_first, position_second, 0.01)
    new_head = adam_step(head_bias, grads[2], head_first, head_second, 0.2)
    new_vec = adam_step(vectors, grads[3], vector_first, vector_second, vector_rates(layers))
    new_inner = adam_step(inner_bias, grads[4], inner_first, inner_second, 0.05)
    new_pool = adam_step(pooler, grads[5], pooler_first, pooler_second, 0.02)
    weight_list = []
    moment_list = []
    for matrix in range(feed_weights.shape[1] // hidden):
        columns = slice(matrix * hidden, (matrix + 1) * hidden)
        moment = muon_keep * feed_moment[:, columns] + grads[6][:, columns]
        ortho = moment / (jnp.sqrt(jnp.sum(moment * moment)) + 1e-07)
        for sweep in range(5):
            gram = jnp.dot(ortho, ortho.T, precision=highest)
            poly = ns_second * gram + ns_third * jnp.dot(gram, gram, precision=highest)
            ortho = ns_first * ortho + jnp.dot(poly, ortho, precision=highest)
        weight_list.append(feed_weights[:, columns] * (1.0 - muon_rate * decay) - muon_rate * 0.2 * math.sqrt(max(width, hidden)) * ortho)
        moment_list.append(moment)
    new_feed = jnp.concatenate(weight_list, axis=1)
    new_moment = jnp.concatenate(moment_list, axis=1)
    return (loss, masked_count, grad_norm, new_emb[0], new_emb[1], new_emb[2], new_pos[0], new_pos[1], new_pos[2], new_head[0], new_head[1], new_head[2], new_vec[0], new_vec[1], new_vec[2], new_inner[0], new_inner[1], new_inner[2], new_pool[0], new_pool[1], new_pool[2], new_feed, new_moment)
```

```python
import math

import jax
import jax.numpy as jnp
import numpy as np
from jax import lax
from jax.sharding import PartitionSpec as P

STEP = 10

highest = lax.Precision.HIGHEST
f32 = jnp.float32
bf16 = jnp.bfloat16
norm_epsilon = 1e-06
beta_one = 0.5
beta_two = 0.5
adam_epsilon = 1e-08
decay = 0.01
clip_limit = 1.0
muon_rate = 0.05
muon_keep = 0.5
ns_first = 3.4445
ns_second = -4.775
ns_third = 2.0315


def vector_rates(layers):
    rates = (
        [0.01, 0.01]
        + [0.2] * (2 * layers + 1)
        + [0.05] * (2 * layers + 1)
        + [0.05] * layers
        + [0.05, 0.02, 0.02]
    )
    return jnp.array(rates, f32)[:, None]


def tie(values):
    return lax.optimization_barrier(values)


def flip(value, bit, axis="seq"):
    return lax.ppermute(value, axis, [(k, k ^ bit) for k in range(lax.axis_size(axis))])


def bits_of(count):
    return [1 << k for k in range(count.bit_length() - 1)]


def ring_order(count):
    return [0] + list(range(1, count, 2)) + list(range(2, count, 2))[::-1]


def ring_place(count):
    order = ring_order(count)
    return [order.index(k) for k in range(count)]


def hop(value):
    count = lax.axis_size("dp")
    order = ring_order(count)
    return lax.ppermute(
        value, "dp", [(order[k], order[(k + 1) % count]) for k in range(count)]
    )


def ring_gather(value):
    out = [value]
    for _ in range(lax.axis_size("dp") - 1):
        out.append(hop(out[-1]))
    return out


def ring_reduce(values):
    count = lax.axis_size("dp")
    index = lax.axis_index("dp")
    order = jnp.array(ring_order(count), jnp.int32)
    place = jnp.array(ring_place(count), jnp.int32)[index]
    held = None
    for step in range(1, count):
        target = order[(place - step) % count]
        mine = lax.dynamic_index_in_dim(values, target, 0, keepdims=False)
        if held is not None:
            mine = (mine.astype(f32) + held.astype(f32)).astype(values.dtype)
        held = hop(mine)
    mine = lax.dynamic_index_in_dim(values, index, 0, keepdims=False)
    return mine.astype(f32) + held.astype(f32)


def plane_keys(count):
    evens = list(range(0, count, 2))
    return evens + [k ^ 1 for k in evens]


def chips_gather(piece):
    count = lax.axis_size("seq")
    if count == 8:
        half = piece.shape[0] // 2
        by_x = flip(piece, 2)
        by_y = flip(piece, 4)
        top = flip(by_x[:half], 4)
        bottom = flip(by_y[half:], 2)
        return jnp.concatenate([piece, by_x, by_y, top, bottom])
    held = piece
    for bit in bits_of(count)[1:]:
        held = jnp.concatenate([held, flip(held, bit)])
    return held


def add_low(left, right):
    return (left.astype(f32) + right.astype(f32)).astype(bf16)


def chips_reduce(held):
    count = lax.axis_size("seq")
    if count == 8:
        half = held.shape[1] // 2
        by_x = flip(held[3, :half], 2)
        by_y = flip(held[3, half:], 4)
        to_y = jnp.concatenate([add_low(held[2, :half], by_x), held[2, half:]])
        to_x = jnp.concatenate([held[1, :half], add_low(held[1, half:], by_y)])
        return held[0].astype(f32) + flip(to_x, 2).astype(f32) + flip(to_y, 4).astype(f32)
    for bit in bits_of(count)[:0:-1]:
        middle = held.shape[0] // 2
        held = add_low(held[:middle], flip(held[middle:], bit))
    return held[0].astype(f32)


def plane_reduce(even, odd):
    return chips_reduce(add_low(even, flip(odd, 1)))


def items_sum(value, first_bit):
    bits = [b for b in bits_of(lax.axis_size("seq")) if b >= first_bit]
    half = value.shape[0] // 2
    top, bottom = value[:half], value[half:]
    for one, other in zip(bits, bits[::-1]):
        top, bottom = (
            add_low(top, flip(top, one)),
            add_low(bottom, flip(bottom, other)),
        )
    return jnp.concatenate([top, bottom])


def everywhere_sum(value):
    for bit in bits_of(lax.axis_size("seq")):
        value = value + flip(value, bit)
    for bit in bits_of(lax.axis_size("dp")):
        value = value + flip(value, bit, "dp")
    return value


def by_distance(values, index):
    return jnp.take(values, jnp.arange(values.shape[0], dtype=jnp.int32) ^ index, axis=0)


def plane_gather_small(value):
    held = value[None]
    for bit in bits_of(lax.axis_size("seq")):
        held = jnp.concatenate([held, flip(held, bit)])
    return by_distance(held, lax.axis_index("seq"))


def tokens_gather(rows):
    count = lax.axis_size("seq")
    rounds = lax.axis_size("dp")
    if count != 8:
        out = []
        for value in ring_gather(rows):
            near = chips_gather(value)
            out.append((near, flip(near, 1)))
        return out
    half = rows.shape[0] // 2
    along, by_x, by_y, near, far = [rows], {}, {}, {}, {}
    for phase in range(rounds + 2):
        new = {}
        if phase < rounds - 1:
            new["z"] = hop(along[phase])
        if phase < rounds:
            new["x"] = flip(along[phase], 2)
            new["y"] = flip(along[phase], 4)
        if 1 <= phase <= rounds:
            new["top"] = flip(by_x[phase - 1][:half], 4)
            new["bottom"] = flip(by_y[phase - 1][half:], 2)
        if phase >= 2:
            new["far"] = flip(near[phase - 2], 1)
        new, along, by_x, by_y, near = tie((new, along, by_x, by_y, near))
        if "z" in new:
            along = along + [new["z"]]
        if "x" in new:
            by_x[phase], by_y[phase] = new["x"], new["y"]
        if "top" in new:
            k = phase - 1
            near[k] = jnp.concatenate([along[k], by_x[k], by_y[k], new["top"], new["bottom"]])
        if "far" in new:
            far[phase - 2] = new["far"]
    return [(near[k], far[k]) for k in range(rounds)]


def dft_constant(length):
    index = np.arange(length, dtype=np.int64)
    phase = (index[:, None] * index[None, :]) % length
    angle = phase.astype(np.float32) * np.float32(2.0 * math.pi / length)
    return np.cos(angle).astype(bf16), np.sin(angle).astype(bf16)


def dft_rows(first_row, row_total, columns, length):
    fine = 32 if row_total % 32 == 0 else 1

    def base(rows):
        phase = (rows[:, None] * columns[None, :]) % length
        angle = phase.astype(f32) * (2.0 * math.pi / length)
        return tie((jnp.cos(angle), jnp.sin(angle)))

    high_cos, high_sin = base(
        first_row + fine * jnp.arange(row_total // fine, dtype=jnp.int32)
    )
    low_cos, low_sin = base(jnp.arange(fine, dtype=jnp.int32))
    cosine = high_cos[:, None] * low_cos[None] - high_sin[:, None] * low_sin[None]
    sine = high_sin[:, None] * low_cos[None] + high_cos[:, None] * low_sin[None]
    shape = (row_total, columns.shape[0])
    return cosine.reshape(shape).astype(bf16), sine.reshape(shape).astype(bf16)


def norm_forward(values):
    centred = values - jnp.mean(values, axis=-1, keepdims=True)
    variance = jnp.mean(centred * centred, axis=-1, keepdims=True)
    scale = lax.rsqrt(variance + norm_epsilon)
    return centred * scale, scale


def norm_backward(grad, unit, scale, gain):
    inward = grad * gain
    average = jnp.mean(inward, axis=-1, keepdims=True)
    along = jnp.mean(inward * unit, axis=-1, keepdims=True)
    return (
        scale * (inward - average - unit * along),
        jnp.sum(grad * unit, axis=0),
        jnp.sum(grad, axis=0),
    )


def gelu_tanh(values):
    return jax.nn.gelu(values, approximate=True)


def dot(left, right, left_dim=1, right_dim=0, precision=None):
    return lax.dot_general(
        left,
        right,
        (((left_dim,), (right_dim,)), ((), ())),
        precision=precision,
        preferred_element_type=f32,
    )


def adam_step(weight, grad, first, second, rate):
    first = beta_one * first + (1.0 - beta_one) * grad
    second = beta_two * second + (1.0 - beta_two) * grad * grad
    first_hat = first / (1.0 - beta_one**STEP)
    second_hat = second / (1.0 - beta_two**STEP)
    weight = weight - rate * (first_hat / (jnp.sqrt(second_hat) + adam_epsilon) + decay * weight)
    return (weight, first, second)


def shards(
    tokens,
    segments,
    masked_pick,
    masked_labels,
    pair_labels,
    embedding,
    embed_first,
    embed_second,
    position_table,
    position_first,
    position_second,
    head_bias,
    head_first,
    head_second,
    vectors,
    vector_first,
    vector_second,
    inner_bias,
    inner_first,
    inner_second,
    pooler,
    pooler_first,
    pooler_second,
    feed_weights,
    feed_moment,
):
    block, items = tokens.shape
    slots = masked_pick.shape[0]
    vocab_rows, width = embedding.shape
    layers, hidden = inner_bias.shape
    norms = 2 * layers + 1
    n_seq = lax.axis_size("seq")
    n_dp = lax.axis_size("dp")
    seq_index = lax.axis_index("seq")
    dp_index = lax.axis_index("dp")
    all_items = items * n_dp
    length = block * n_seq
    shares = n_seq // items
    count = length // shares
    own_item = seq_index // shares
    own_part = seq_index % shares
    keys = np.array(plane_keys(n_seq), np.int32)
    order = jnp.array(ring_order(n_dp), jnp.int32)
    places = jnp.array(ring_place(n_dp), jnp.int32)
    place = places[dp_index]
    columns = feed_weights.shape[1]

    feed_piece = ring_gather(feed_weights.astype(bf16).T)
    feed_piece = jnp.stack(feed_piece)

    integers = jnp.concatenate([tokens.reshape(-1), segments.reshape(-1), masked_pick.reshape(-1)])
    group = plane_gather_small(integers)

    def by_share(flat):
        return flat.reshape(n_seq, block, items).transpose(2, 0, 1).reshape(n_seq, count)

    size = block * items
    group_tokens = by_share(group[:, :size])
    own_segments = lax.dynamic_index_in_dim(
        by_share(group[:, size : 2 * size]), seq_index, 0, keepdims=False
    )
    picks = group[:, 2 * size :].reshape(shares, n_seq // shares * slots)
    picks = lax.dynamic_index_in_dim(picks, own_part, 0, keepdims=False)

    emb_low = embedding.astype(bf16)
    look_table = jnp.concatenate([emb_low, position_table.astype(bf16)])
    targets = jnp.asarray(keys) ^ seq_index
    wanted = jnp.take(group_tokens, targets, axis=0) - seq_index * vocab_rows
    at = (targets % shares)[:, None] * count + jnp.arange(count, dtype=jnp.int32)[None, :]
    at = at - seq_index * block
    wanted = jnp.where((wanted >= 0) & (wanted < vocab_rows), wanted, -1)
    at = jnp.where((at >= 0) & (at < block), at + vocab_rows, -1)

    def looked(part):
        rows = jnp.arange(vocab_rows + block, dtype=jnp.int32)
        hot = (wanted[part].reshape(-1)[:, None] == rows) | (at[part].reshape(-1)[:, None] == rows)
        found = dot(hot.astype(bf16), look_table)
        return found.astype(bf16).reshape(n_seq // 2, count, width)

    odd_rows = looked(slice(n_seq // 2, n_seq))
    even_rows = looked(slice(0, n_seq // 2))
    embedded = plane_reduce(even_rows, odd_rows)
    embedded = embedded + jnp.where(own_segments[:, None] == 1, vectors[1], vectors[0])

    cos_hid, sin_hid = dft_constant(width)
    cos_hid, sin_hid = jnp.asarray(cos_hid), jnp.asarray(sin_hid)
    sources = own_part ^ jnp.arange(shares, dtype=jnp.int32)
    table_columns = (
        sources[:, None] * count + jnp.arange(count, dtype=jnp.int32)[None, :]
    ).reshape(-1)
    cos_seq, sin_seq = dft_rows(own_part * count, count, table_columns, length)

    feed_all = []
    held_back = None
    for matrix in range(n_dp):
        piece = lax.dynamic_index_in_dim(
            feed_piece, (place - places[matrix]) % n_dp, 0, keepdims=False
        )
        if held_back is not None:
            piece, held_back = tie((piece, held_back))
            feed_all.append((held_back, flip(held_back, 1)))
        held_back = chips_gather(piece)
    feed_all.append((held_back, flip(held_back, 1)))
    feed_all = [jnp.concatenate(pair) for pair in feed_all]

    bias_rel = jnp.take(
        inner_bias.reshape(layers, n_seq, hidden // n_seq), targets, axis=1
    ).reshape(layers, hidden)

    def share_gather(value):
        held = value[None]
        for bit in bits_of(shares):
            held = jnp.concatenate([held, flip(held, bit)])
        return held

    def mix_forward(stream_low):
        pair = jnp.stack([dot(stream_low, cos_hid), dot(stream_low, sin_hid)]).astype(bf16)
        held = share_gather(pair)
        part_a = held[:, 0].reshape(length, width)
        part_b = held[:, 1].reshape(length, width)
        return (dot(cos_seq, part_a) - dot(sin_seq, part_b)).astype(bf16)

    def mix_backward(grad_low):
        held = share_gather(grad_low).reshape(length, width)
        part_a = dot(cos_seq, held).astype(bf16)
        part_b = (-dot(sin_seq, held)).astype(bf16)
        return dot(part_a, cos_hid) + dot(part_b, sin_hid)

    unit_zero, scale_zero = norm_forward(embedded)
    stream = unit_zero * vectors[2] + vectors[2 + norms]
    saved = []
    for layer in range(layers):
        w_in, w_out = feed_all[2 * layer], feed_all[2 * layer + 1]
        gain_a, shift_a = vectors[3 + 2 * layer], vectors[3 + 2 * layer + norms]
        gain_b, shift_b = vectors[4 + 2 * layer], vectors[4 + 2 * layer + norms]
        mixed = mix_forward(stream.astype(bf16))
        unit_a, scale_a = norm_forward(stream + mixed.astype(f32))
        joined = unit_a * gain_a + shift_a
        joined_low = joined.astype(bf16)
        inner = dot(joined_low, w_in, 1, 1) + bias_rel[layer]
        active_low = gelu_tanh(inner).astype(bf16)
        output = dot(active_low, w_out) + vectors[2 + 2 * norms + layer]
        unit_b, scale_b = norm_forward(joined + output)
        stream = unit_b * gain_b + shift_b
        saved.append((joined_low, inner, active_low, unit_a, scale_a, unit_b, scale_b))

    row_at = jnp.arange(n_seq // shares, dtype=jnp.int32)[:, None] * block + (
        picks.reshape(n_seq // shares, slots) // items
    )
    row_at = jnp.where(picks % items == own_item, row_at.reshape(-1), -1)
    chosen = (row_at[:, None] == jnp.arange(count, dtype=jnp.int32)).astype(bf16)
    masked_part = items_sum(dot(chosen, stream.astype(bf16)).astype(bf16), shares)
    masked_rows = by_distance(share_gather(masked_part), own_part).reshape(n_seq * slots, width)

    pool_row = 2 + 2 * norms + layers
    leads = (own_part == 0).astype(f32)
    label = lax.dynamic_index_in_dim(pair_labels, own_item, 0, keepdims=False)

    def pair_loss(first_row, pool_shift, class_rows):
        pooled = jnp.tanh(jnp.dot(first_row, pooler, precision=highest) + pool_shift)
        scores = jnp.sum(pooled * class_rows, axis=1)
        top_score = jnp.max(scores)
        log_sum = top_score + jnp.log(jnp.sum(jnp.exp(scores - top_score)))
        return log_sum - jnp.sum(jnp.where(jnp.arange(2) == label, scores, 0.0))

    first_row = stream[:1]
    pair_value, pair_back = jax.vjp(
        pair_loss, first_row, vectors[pool_row][None], vectors[pool_row + 1 : pool_row + 3]
    )
    d_first_row, d_pool_shift, d_class = pair_back(leads / all_items)

    labels = lax.dynamic_index_in_dim(masked_labels, dp_index, 1, keepdims=False)
    masked_count = jnp.sum(masked_labels >= 0).astype(f32)
    logits = dot(masked_rows, emb_low, 1, 1) + head_bias
    vocab_ids = seq_index * vocab_rows + jnp.arange(vocab_rows, dtype=jnp.int32)
    is_target = labels[:, None] == vocab_ids[None, :]
    peak = jnp.max(logits, axis=1)
    totals = jnp.sum(jnp.exp(logits - peak[:, None]), axis=1)
    target = jnp.sum(jnp.where(is_target, logits, 0.0), axis=1)
    stats = plane_gather_small(jnp.stack([peak, totals, target]))
    peak_all = jnp.max(stats[:, 0], axis=0)
    log_total = peak_all + jnp.log(jnp.sum(stats[:, 1] * jnp.exp(stats[:, 0] - peak_all), axis=0))
    target_all = jnp.sum(stats[:, 2], axis=0)
    counted = labels >= 0
    leader = (seq_index == 0).astype(f32)
    masked_local = leader * jnp.sum(jnp.where(counted, log_total - target_all, 0.0))
    weighting = jnp.where(counted, 1.0 / masked_count, 0.0)
    d_logits = (jnp.exp(logits - log_total[:, None]) - is_target.astype(f32)) * weighting[:, None]
    d_head_bias = jnp.sum(d_logits, axis=0)
    d_logits_low = d_logits.astype(bf16)
    d_rows = dot(d_logits_low, emb_low).astype(bf16)
    d_rows = by_distance(d_rows.reshape(shares, n_seq // shares * slots, width), own_part)
    for bit in bits_of(shares)[::-1]:
        middle = d_rows.shape[0] // 2
        d_rows = add_low(d_rows[:middle], flip(d_rows[middle:], bit))
    d_rows = items_sum(d_rows[0], shares)
    d_stream = dot(chosen, d_rows, 0, 0)
    d_stream = d_stream.at[:1].add(d_first_row)

    quarter = -(-vocab_rows // (16 * n_dp)) * 16
    d_embed_head = dot(d_logits_low, masked_rows, 0, 0).astype(bf16)
    d_embed_head = jnp.pad(d_embed_head, ((0, quarter * n_dp - vocab_rows), (0, 0)))
    d_embed_head = ring_reduce(d_embed_head.reshape(n_dp, quarter, width))
    for bit in bits_of(n_dp):
        d_head_bias = d_head_bias + flip(d_head_bias, bit, "dp")

    all_tokens = group_tokens[None]
    for bit in bits_of(n_dp):
        all_tokens = jnp.concatenate([all_tokens, flip(all_tokens, bit, "dp")])
    all_tokens = by_distance(all_tokens, dp_index)

    layer_grads = [None] * layers
    feed_grads = [None] * (2 * layers)
    halves = (n_seq // 2, hidden // n_seq, width)

    def to_owner(grad):
        grad = grad.astype(bf16)
        return plane_reduce(
            grad[: hidden // 2].reshape(halves), grad[hidden // 2 :].reshape(halves)
        ).astype(bf16)

    for layer in reversed(range(layers)):
        joined_low, inner, active_low, unit_a, scale_a, unit_b, scale_b = saved[layer]
        w_in, w_out = feed_all[2 * layer], feed_all[2 * layer + 1]
        d_second, d_gain_b, d_shift_b = norm_backward(
            d_stream, unit_b, scale_b, vectors[4 + 2 * layer]
        )
        d_bias_out = jnp.sum(d_second, axis=0)
        d_out_low = d_second.astype(bf16)
        feed_grads[2 * layer + 1] = to_owner(dot(active_low, d_out_low, 0, 0))
        d_active = dot(d_out_low, w_out, 1, 1)
        (d_inner,) = jax.vjp(gelu_tanh, inner)[1](d_active)
        d_bias_in = jnp.sum(d_inner, axis=0)
        d_in_low = d_inner.astype(bf16)
        feed_grads[2 * layer] = to_owner(dot(d_in_low, joined_low, 0, 0))
        d_joined = d_second + dot(d_in_low, w_in)
        d_first, d_gain_a, d_shift_a = norm_backward(
            d_joined, unit_a, scale_a, vectors[3 + 2 * layer]
        )
        d_stream = d_first + mix_backward(d_first.astype(bf16))
        layer_grads[layer] = (d_bias_in, d_bias_out, d_gain_a, d_shift_a, d_gain_b, d_shift_b)
    d_embedded, d_gain_zero, d_shift_zero = norm_backward(
        d_stream, unit_zero, scale_zero, vectors[2]
    )
    is_second = (own_segments == 1)[:, None]
    d_type_zero = jnp.sum(jnp.where(is_second, 0.0, d_embedded), axis=0)
    d_type_one = jnp.sum(jnp.where(is_second, d_embedded, 0.0), axis=0)

    gathered = tokens_gather(d_embedded.astype(bf16))
    rows = jnp.arange(quarter + block, dtype=jnp.int32)
    row_base = seq_index * vocab_rows + dp_index * quarter
    row_end = jnp.minimum(row_base + quarter, (seq_index + 1) * vocab_rows)
    d_token = None
    for k in range(n_dp):
        group_index = order[(place - k) % n_dp]
        of_group = lax.dynamic_index_in_dim(all_tokens, group_index, 0, keepdims=False)
        for side in range(2):
            devices = jnp.asarray(keys[side * n_seq // 2 : (side + 1) * n_seq // 2]) ^ seq_index
            ids = jnp.take(of_group, devices, axis=0)
            ids = jnp.where((ids >= row_base) & (ids < row_end), ids - row_base, -1)
            at = (devices % shares)[:, None] * count + jnp.arange(count, dtype=jnp.int32)
            at = at - seq_index * block
            at = jnp.where((at >= 0) & (at < block), at + quarter, -1)
            hot = (rows[:, None] == ids.reshape(-1)) | (rows[:, None] == at.reshape(-1))
            part = dot(hot.astype(bf16), gathered[k][side])
            d_token = part if d_token is None else d_token + part
    d_embed_own = d_token[:quarter] + d_embed_head
    d_position = d_token[quarter:]

    feed_grad = ring_reduce(jnp.stack(feed_grads)).T

    gain_rows, shift_rows = [d_gain_zero], [d_shift_zero]
    out_rows, inner_rows = [], []
    for layer in range(layers):
        d_bias_in, d_bias_out, d_gain_a, d_shift_a, d_gain_b, d_shift_b = layer_grads[layer]
        gain_rows += [d_gain_a, d_gain_b]
        shift_rows += [d_shift_a, d_shift_b]
        out_rows.append(d_bias_out)
        inner_rows.append(d_bias_in)
    d_vectors = jnp.stack(
        [d_type_zero, d_type_one]
        + gain_rows
        + shift_rows
        + out_rows
        + [d_pool_shift[0], d_class[0], d_class[1]]
    )
    spots = np.argsort(keys).astype(np.int32)
    d_inner = jnp.take(
        jnp.stack(inner_rows).reshape(layers, n_seq, hidden // n_seq),
        jnp.asarray(spots)[jnp.arange(n_seq, dtype=jnp.int32) ^ seq_index],
        axis=1,
    ).reshape(layers, hidden)
    mine = (jnp.arange(all_items) == dp_index * items + own_item)[:, None] & (own_part == 0)
    small = jnp.concatenate(
        [
            d_vectors.reshape(-1),
            d_inner.reshape(-1),
            jnp.where(mine, first_row, 0.0).reshape(-1),
            jnp.where(mine, d_pool_shift, 0.0).reshape(-1),
            jnp.stack([masked_local, leads * pair_value]),
            jnp.zeros((width - 2,), f32),
        ]
    ).reshape(-1, width)
    small = everywhere_sum(small)
    vector_count = vectors.shape[0]
    inner_count = layers * hidden // width
    d_vectors = small[:vector_count]
    d_inner = small[vector_count : vector_count + inner_count].reshape(layers, hidden)
    rest = small[vector_count + inner_count :]
    d_pooler = dot(rest[:all_items], rest[all_items : 2 * all_items], 0, 0, highest)
    masked_sum, pair_sum = rest[2 * all_items, 0], rest[2 * all_items, 1]

    dp_leader = (dp_index == 0).astype(f32)
    spread_squares = (
        jnp.sum(feed_grad * feed_grad)
        + jnp.sum(d_embed_own * d_embed_own)
        + dp_leader * (jnp.sum(d_position * d_position) + jnp.sum(d_head_bias * d_head_bias))
    )
    small_squares = (
        jnp.sum(d_vectors * d_vectors) + jnp.sum(d_inner * d_inner) + jnp.sum(d_pooler * d_pooler)
    )
    spread_squares = everywhere_sum(spread_squares.reshape(1, 1))[0, 0]
    grad_norm = jnp.sqrt(spread_squares + small_squares)
    clip = clip_limit / jnp.maximum(grad_norm, clip_limit)
    loss = masked_sum / masked_count + pair_sum / all_items

    quarters = jnp.stack(ring_gather(d_embed_own.astype(bf16)))
    d_embed = jnp.concatenate(
        [
            lax.dynamic_index_in_dim(quarters, (place - places[k]) % n_dp, 0, keepdims=False)
            for k in range(n_dp)
        ]
    )[:vocab_rows].astype(f32)
    new_emb = adam_step(embedding, d_embed * clip, embed_first, embed_second, 0.02)
    new_pos = adam_step(position_table, d_position * clip, position_first, position_second, 0.01)
    new_head = adam_step(head_bias, d_head_bias * clip, head_first, head_second, 0.2)
    new_vec = adam_step(
        vectors, d_vectors * clip, vector_first, vector_second, vector_rates(layers)
    )
    new_inner = adam_step(inner_bias, d_inner * clip, inner_first, inner_second, 0.05)
    new_pool = adam_step(pooler, d_pooler * clip, pooler_first, pooler_second, 0.02)

    moment = muon_keep * feed_moment + clip * feed_grad
    gram = dot(moment, moment, 1, 1, highest)
    for bit in bits_of(n_seq):
        gram = gram + flip(gram, bit)
    scaling = 1.0 / (jnp.sqrt(jnp.trace(gram)) + 1e-07)
    gram = gram * (scaling * scaling)
    unit = jnp.eye(width, dtype=f32)
    total = None
    for sweep in range(5):
        poly = ns_first * unit + ns_second * gram + ns_third * dot(gram, gram, 1, 0, highest)
        total = poly if total is None else dot(poly, total, 1, 0, highest)
        if sweep < 4:
            gram = dot(poly, dot(poly, gram, 1, 0, highest), 1, 0, highest)
    ortho = dot(total, moment * scaling, 1, 0, highest)
    new_feed = (
        feed_weights * (1.0 - muon_rate * decay)
        - muon_rate * 0.2 * math.sqrt(max(width, hidden)) * ortho
    )
    return (
        loss,
        masked_count,
        grad_norm,
        new_emb[0],
        new_emb[1],
        new_emb[2],
        new_pos[0],
        new_pos[1],
        new_pos[2],
        new_head[0],
        new_head[1],
        new_head[2],
        new_vec[0],
        new_vec[1],
        new_vec[2],
        new_inner[0],
        new_inner[1],
        new_inner[2],
        new_pool[0],
        new_pool[1],
        new_pool[2],
        new_feed,
        moment,
    )


def solution(mesh):
    return jax.shard_map(
        shards,
        mesh=mesh,
        in_specs=(
            P("seq", "dp"),
            P("seq", "dp"),
            P("seq", "dp"),
            P(),
            P("dp"),
            P("seq", None),
            P("seq", None),
            P("seq", None),
            P("seq", None),
            P("seq", None),
            P("seq", None),
            P("seq"),
            P("seq"),
            P("seq"),
            P(),
            P(),
            P(),
            P(),
            P(),
            P(),
            P(),
            P(),
            P(),
            P(None, ("dp", "seq")),
            P(None, ("dp", "seq")),
        ),
        out_specs=(
            P(),
            P(),
            P(),
            P("seq", None),
            P("seq", None),
            P("seq", None),
            P("seq", None),
            P("seq", None),
            P("seq", None),
            P("seq"),
            P("seq"),
            P("seq"),
            P(),
            P(),
            P(),
            P(),
            P(),
            P(),
            P(),
            P(),
            P(),
            P(None, ("dp", "seq")),
            P(None, ("dp", "seq")),
        ),
        check_vma=False,
    )
```

```python
import functools
import math

import jax
import jax.numpy as jnp
import numpy as np
from jax import lax
from jax.experimental import pallas as pl
from jax.experimental.layout import Layout, with_layout_constraint
from jax.experimental.pallas import tpu as pltpu
from jax.sharding import PartitionSpec as P

STEP = 10

highest = lax.Precision.HIGHEST
high = lax.Precision.HIGH
f32 = jnp.float32
bf16 = jnp.bfloat16
norm_epsilon = 1e-06
beta_one = 0.5
beta_two = 0.5
adam_epsilon = 1e-08
decay = 0.01
clip_limit = 1.0
muon_rate = 0.05
muon_keep = 0.5
ns_first = 3.4445
ns_second = -4.775
ns_third = 2.0315


def vector_rates(layers):
    rates = (
        [0.01, 0.01]
        + [0.2] * (2 * layers + 1)
        + [0.05] * (2 * layers + 1)
        + [0.05] * layers
        + [0.05, 0.02, 0.02]
    )
    return jnp.array(rates, f32)[:, None]


def tie(values):
    return lax.optimization_barrier(values)


def flip(value, bit, axis="seq"):
    return lax.ppermute(value, axis, [(k, k ^ bit) for k in range(lax.axis_size(axis))])


def bits_of(count):
    return [1 << k for k in range(count.bit_length() - 1)]


def ring_order(count):
    return [0] + list(range(1, count, 2)) + list(range(2, count, 2))[::-1]


def ring_place(count):
    order = ring_order(count)
    return [order.index(k) for k in range(count)]


def hop(value):
    count = lax.axis_size("dp")
    order = ring_order(count)
    return lax.ppermute(
        value, "dp", [(order[k], order[(k + 1) % count]) for k in range(count)]
    )


def ring_gather(value):
    out = [value]
    for _ in range(lax.axis_size("dp") - 1):
        out.append(hop(out[-1]))
    return out


def plane_keys(count):
    evens = list(range(0, count, 2))
    return evens + [k ^ 1 for k in evens]


def rowwise(value):
    return with_layout_constraint(value, Layout(tuple(range(value.ndim))))


along_dp = 0
few_rows = 384


def exchange(channel, value):
    return hop(value) if channel == along_dp else flip(value, channel)


def run(*tasks):
    results = [None] * len(tasks)
    live = dict(enumerate(tasks))
    replies = {}
    number = 0
    while live:
        sends, keeps = {}, {}
        for name, (first, task) in list(live.items()):
            if number < first:
                continue
            try:
                asked, keeps[name] = task.send(replies.get(name))
            except StopIteration as end:
                results[name] = end.value
                del live[name]
                continue
            for channel, parts in asked.items():
                sends.setdefault(channel, []).extend((name, part) for part in parts)
        came = {}
        for channel, parts in sends.items():
            few = [k for k, (_, part) in enumerate(parts) if part.shape[0] <= few_rows]
            came[channel] = {
                k: exchange(channel, part)
                for k, (_, part) in enumerate(parts)
                if k not in few or len(few) == 1
            }
            if len(few) > 1:
                came[channel]["few"] = exchange(
                    channel, jnp.concatenate([parts[k][1] for k in few])
                )
        came = [list(group.items()) for group in came.values()]
        labels = [[key for key, _ in group] for group in came]
        came = [[value for _, value in group] for group in came]
        came, keeps = tie((came, keeps)) if keeps else (came, keeps)
        came = {
            channel: dict(zip(names, group))
            for channel, names, group in zip(sends, labels, came)
        }
        replies = {name: ({}, kept) for name, kept in keeps.items()}
        for channel, parts in sends.items():
            start = 0
            for k, (name, part) in enumerate(parts):
                if k in came[channel]:
                    got = came[channel][k]
                else:
                    got = came[channel]["few"][start : start + part.shape[0]]
                    start += part.shape[0]
                replies[name][0].setdefault(channel, []).append(got)
        number += 1
    return results


def beside(*tasks):
    results = [None] * len(tasks)
    live = dict(enumerate(tasks))
    replies = {}
    while live:
        sends, keeps, counts = {}, {}, {}
        for name, task in list(live.items()):
            try:
                asked, keeps[name] = task.send(replies.get(name))
            except StopIteration as end:
                results[name] = end.value
                del live[name]
                continue
            for channel, parts in asked.items():
                sends.setdefault(channel, []).extend(parts)
                counts.setdefault(channel, []).extend([name] * len(parts))
        if not live:
            break
        came, keeps = yield sends, keeps
        replies = {name: ({}, kept) for name, kept in keeps.items()}
        for channel, names in counts.items():
            for name, part in zip(names, came[channel]):
                replies[name][0].setdefault(channel, []).append(part)
    return results


def plane_gather(piece):
    count = lax.axis_size("seq")
    if count == 8:
        half = piece.shape[0] // 2
        came, piece = yield {2: [piece], 4: [piece]}, piece
        by_x, by_y = came[2][0], came[4][0]
        came, kept = yield {4: [by_x[:half]], 2: [by_y[half:]]}, (piece, by_x, by_y)
        held = jnp.concatenate([*kept, came[4][0], came[2][0]])
    else:
        held = piece
        for bit in bits_of(count)[1:]:
            came, held = yield {bit: [held]}, held
            held = jnp.concatenate([held, came[bit][0]])
    return held, flip(held, 1)


def add_low(left, right):
    return (left.astype(f32) + right.astype(f32)).astype(bf16)


def chips_reduce(held):
    count = lax.axis_size("seq")
    if count == 8:
        half = held[0].shape[0] // 2
        came, held = yield {2: [held[3][:half]], 4: [held[3][half:]]}, held
        to_y = jnp.concatenate([add_low(held[2][:half], came[2][0]), held[2][half:]])
        to_x = jnp.concatenate([held[1][:half], add_low(held[1][half:], came[4][0])])
        came, mine = yield {2: [to_x], 4: [to_y]}, held[0]
        return mine.astype(f32) + came[2][0].astype(f32) + came[4][0].astype(f32)
    for bit in bits_of(count)[:0:-1]:
        middle = len(held) // 2
        came, held = yield {bit: held[middle:]}, held[:middle]
        held = [add_low(one, two) for one, two in zip(held, came[bit])]
    return held[0].astype(f32)


def plane_reduce(even, odd):
    came, even = yield {1: [odd.reshape(-1, odd.shape[-1])]}, even
    held = add_low(even, came[1][0].reshape(odd.shape))
    return (yield from chips_reduce([held[k] for k in range(held.shape[0])]))


def ring_reduce(values, waits=()):
    count = lax.axis_size("dp")
    index = lax.axis_index("dp")
    order = ring_order(count)
    place = chosen_of(ring_place(count), index)
    held = None
    for step in range(1, count):
        mine = lax.dynamic_index_in_dim(values, chosen_of(order, (place - step) % count), 0, keepdims=False)
        if held is not None:
            mine = add_low(mine, held)
        wait = waits[step - 1] if waits else 0
        if wait:
            held = hop(mine)
            for _ in range(wait):
                _, values = yield {}, values
            _, (values, held) = yield {}, (values, held)
        else:
            came, values = yield {along_dp: [mine]}, values
            held = came[along_dp][0]
    mine = lax.dynamic_index_in_dim(values, index, 0, keepdims=False)
    return mine.astype(f32) + held.astype(f32)


def split_low(value):
    top = lax.reduce_precision(value, 8, 7)
    return jnp.concatenate([top.astype(bf16), (value - top).astype(bf16)])


def join_low(value):
    middle = value.shape[0] // 2
    return value[:middle].astype(f32) + value[middle:].astype(f32)


def reduce_everywhere(value):
    for bit in bits_of(lax.axis_size("seq")):
        low = split_low(value)
        came, low = yield {bit: [low]}, low
        value = join_low(low) + join_low(came[bit][0])
    low = [split_low(value)]
    for _ in range(lax.axis_size("dp") - 1):
        came, low = yield {along_dp: [low[-1]]}, low
        low = low + [came[along_dp][0]]
    count = lax.axis_size("dp")
    places = ring_place(count)
    place = chosen_of(places, lax.axis_index("dp"))
    stacked = jnp.stack([join_low(part) for part in low])
    total = None
    for k in range(count):
        part = lax.dynamic_index_in_dim(stacked, (place - places[k]) % count, 0, keepdims=False)
        total = part if total is None else total + part
    return total


def square_sum(square):
    width = square.shape[0]
    part = width // 3
    pairs = [(0, 0), (0, 1), (0, 2), (1, 1), (1, 2), (2, 2)]
    blocks = [square[a * part : (a + 1) * part, b * part : (b + 1) * part] for a, b in pairs]
    held = jnp.concatenate(blocks)
    index = lax.axis_index("seq")

    def halve(value, bit):
        side = (index & bit) // bit
        middle = value.shape[0] // 2
        mine = lax.dynamic_slice_in_dim(value, side * middle, middle)
        other = lax.dynamic_slice_in_dim(value, (1 - side) * middle, middle)
        return mine + flip(other, bit)

    def join(value, bit):
        other = flip(value, bit)
        low = (index & bit) == 0
        return jnp.concatenate([jnp.where(low, value, other), jnp.where(low, other, value)])

    bits = bits_of(lax.axis_size("seq"))
    held = halve(held, 1)
    middle = held.shape[0] // 2
    one, two = held[:middle], held[middle:]
    for bit, other in zip(bits[1:], bits[:0:-1]):
        one, two = one + flip(one, bit), two + flip(two, other)
    held = jnp.concatenate([one, two])
    held = join(held, 1)
    found = {}
    for k, (a, b) in enumerate(pairs):
        block = held[k * part : (k + 1) * part]
        found[a, b] = block
        if a != b:
            found[b, a] = block.T
    return jnp.concatenate(
        [jnp.concatenate([found[a, b] for b in range(3)], axis=1) for a in range(3)]
    )


def items_sum(value, first_bit):
    bits = [b for b in bits_of(lax.axis_size("seq")) if b >= first_bit]
    half = value.shape[0] // 2
    top, bottom = value[:half], value[half:]
    for one, other in zip(bits, bits[::-1]):
        top, bottom = (
            add_low(top, flip(top, one)),
            add_low(bottom, flip(bottom, other)),
        )
    return jnp.concatenate([top, bottom])


def by_distance(values, index):
    count = values.shape[0]
    for bit in bits_of(count):
        pairs = values.reshape((count // (2 * bit), 2, bit) + values.shape[1:])
        swapped = jnp.concatenate([pairs[:, 1:], pairs[:, :1]], axis=1).reshape(values.shape)
        values = jnp.where(index & bit > 0, swapped, values)
    return values


def chosen_of(table, index):
    found = jnp.int32(table[0])
    for k, value in enumerate(table[1:], 1):
        found = jnp.where(index == k, jnp.int32(value), found)
    return found


def row_of(values, index):
    spots = jnp.arange(values.shape[0]).reshape((-1,) + (1,) * (values.ndim - 1))
    return jnp.sum(jnp.where(spots == index, values, 0), axis=0)


def plane_gather_small(value):
    held = value[None]
    for bit in bits_of(lax.axis_size("seq")):
        held = jnp.concatenate([held, flip(held, bit)])
    return by_distance(held, lax.axis_index("seq"))


def dft_constant(length):
    index = np.arange(length, dtype=np.int64)
    phase = (index[:, None] * index[None, :]) % length
    angle = phase.astype(np.float32) * np.float32(2.0 * math.pi / length)
    return np.cos(angle).astype(bf16), np.sin(angle).astype(bf16)


def dft_rows(first_row, row_total, columns, length):
    fine = 32 if row_total % 32 == 0 else 1

    def base(rows):
        phase = (rows[:, None] * columns[None, :]) % length
        angle = phase.astype(f32) * (2.0 * math.pi / length)
        return tie((jnp.cos(angle), jnp.sin(angle)))

    high_cos, high_sin = base(
        first_row + fine * jnp.arange(row_total // fine, dtype=jnp.int32)
    )
    low_cos, low_sin = base(jnp.arange(fine, dtype=jnp.int32))
    cosine = high_cos[:, None] * low_cos[None] - high_sin[:, None] * low_sin[None]
    sine = high_sin[:, None] * low_cos[None] + high_cos[:, None] * low_sin[None]
    shape = (row_total, columns.shape[0])
    return cosine.reshape(shape).astype(bf16), sine.reshape(shape).astype(bf16)


def norm_forward(values):
    centred = values - jnp.mean(values, axis=-1, keepdims=True)
    variance = jnp.mean(centred * centred, axis=-1, keepdims=True)
    scale = lax.rsqrt(variance + norm_epsilon)
    return centred * scale, scale


def norm_backward(grad, unit, scale, gain):
    inward = grad * gain
    average = jnp.mean(inward, axis=-1, keepdims=True)
    along = jnp.mean(inward * unit, axis=-1, keepdims=True)
    return (
        scale * (inward - average - unit * along),
        jnp.sum(grad * unit, axis=0),
        jnp.sum(grad, axis=0),
    )


def gelu_tanh(values):
    return jax.nn.gelu(values, approximate=True)


def dot(left, right, left_dim=1, right_dim=0, precision=None):
    return lax.dot_general(
        left,
        right,
        (((left_dim,), (right_dim,)), ((), ())),
        precision=precision,
        preferred_element_type=f32,
    )


def sweeps_kernel(part, coefficients, opening, *refs):
    if opening:
        gram_ref, out_ref, gram_s, poly_s, hold_s, left_s, right_s = refs
    else:
        gram_ref, so_far_ref, out_ref, gram_s, poly_s, hold_s, left_s, right_s = refs
    first, second, third = coefficients
    width = gram_ref.shape[0]
    blocks = width // part

    def pieces(value, count):
        out = []
        for _ in range(count):
            low = value.astype(jnp.bfloat16)
            out.append(low)
            value = value - low.astype(jnp.float32)
        return out

    def load(ref, side, source, terms):
        for row in range(blocks):
            rows = pl.ds(row * part, part)
            parts = pieces(source[rows, :], 1 + max(terms))
            for spot, term in enumerate(terms):
                if side == 0:
                    ref[rows, spot * width : (spot + 1) * width] = parts[term]
                else:
                    ref[pl.ds(spot * width + row * part, part), :] = parts[term]

    def product(target, more=False):
        for column in range(blocks):
            high = (column + 1) * part
            cols = slice(column * part, high)
            value = jnp.dot(
                left_s[:high, :], right_s[:, cols], preferred_element_type=jnp.float32
            )
            if more:
                value = value + target[:high, cols]
            target[:high, cols] = value
            for row in range(column):
                rows = slice(row * part, (row + 1) * part)
                target[cols, rows] = value[rows].T

    coarse = ((0, 1, 0), (0, 0, 1))
    rest = ((1, 0, 2), (1, 2, 0))

    def times(target, left, right, fine=False):
        load(left_s, 0, left, coarse[0])
        load(right_s, 1, right, coarse[1])
        product(target)
        if fine:
            load(left_s, 0, left, rest[0])
            load(right_s, 1, right, rest[1])
            product(target, True)

    def make_poly(fine=False):
        times(hold_s, gram_s, gram_s, fine)
        for row in range(blocks):
            rows = pl.ds(row * part, part)
            spot = lax.broadcasted_iota(jnp.int32, (part, width), 0) + row * part
            unit = spot == lax.broadcasted_iota(jnp.int32, (part, width), 1)
            poly_s[rows, :] = (
                jnp.where(unit, first, 0.0) + second * gram_s[rows, :] + third * hold_s[rows, :]
            )

    def next_gram(fine=False):
        times(hold_s, poly_s, gram_s, fine)
        times(gram_s, poly_s, hold_s, fine)

    def next_out():
        times(hold_s, poly_s, out_ref)
        out_ref[...] = hold_s[...]

    gram_s[...] = gram_ref[...]
    if opening:
        make_poly(True)
        out_ref[...] = poly_s[...]
        next_gram(True)
        make_poly()
        next_out()
        next_gram()
        return
    out_ref[...] = so_far_ref[...]

    @pl.loop(0, 2)
    def _(_):
        make_poly()
        next_out()
        next_gram()

    make_poly()
    next_out()


def sweeps(gram, so_far=None):
    width = gram.shape[0]
    opening = so_far is None
    square = jax.ShapeDtypeStruct((width, width), jnp.float32)
    scratch = pltpu.VMEM((width, width), jnp.float32)
    whole = pl.BlockSpec(memory_space=pltpu.VMEM)
    return pl.pallas_call(
        functools.partial(
            sweeps_kernel, width // 3, (ns_first, ns_second, ns_third), opening
        ),
        out_shape=[square, square] if opening else square,
        in_specs=[whole] if opening else [whole, whole],
        out_specs=[whole, whole] if opening else whole,
        scratch_shapes=([] if opening else [scratch])
        + [
            scratch,
            scratch,
            pltpu.VMEM((width, 3 * width), jnp.bfloat16),
            pltpu.VMEM((3 * width, width), jnp.bfloat16),
        ],
        compiler_params=pltpu.CompilerParams(vmem_limit_bytes=44 << 20),
        cost_estimate=pl.CostEstimate(
            flops=60 * width**3, bytes_accessed=16 * width * width, transcendentals=0
        ),
    )(*([gram] if opening else [gram, so_far]))


def adam_step(weight, grad, first, second, rate):
    first = beta_one * first + (1.0 - beta_one) * grad
    second = beta_two * second + (1.0 - beta_two) * grad * grad
    first_hat = first / (1.0 - beta_one**STEP)
    second_hat = second / (1.0 - beta_two**STEP)
    weight = weight - rate * (first_hat / (jnp.sqrt(second_hat) + adam_epsilon) + decay * weight)
    return (weight, first, second)


def shards(
    tokens,
    segments,
    masked_pick,
    masked_labels,
    pair_labels,
    embedding,
    embed_first,
    embed_second,
    position_table,
    position_first,
    position_second,
    head_bias,
    head_first,
    head_second,
    vectors,
    vector_first,
    vector_second,
    inner_bias,
    inner_first,
    inner_second,
    pooler,
    pooler_first,
    pooler_second,
    feed_weights,
    feed_moment,
):
    block, items = tokens.shape
    slots = masked_pick.shape[0]
    vocab_rows, width = embedding.shape
    layers, hidden = inner_bias.shape
    norms = 2 * layers + 1
    n_seq = lax.axis_size("seq")
    n_dp = lax.axis_size("dp")
    seq_index = lax.axis_index("seq")
    dp_index = lax.axis_index("dp")
    all_items = items * n_dp
    length = block * n_seq
    shares = n_seq // items
    count = length // shares
    own_item = seq_index // shares
    own_part = seq_index % shares
    keys = np.array(plane_keys(n_seq), np.int32)
    order = ring_order(n_dp)
    places = ring_place(n_dp)
    place = chosen_of(places, dp_index)
    quarter = -(-vocab_rows // (16 * n_dp)) * 16

    feed_own = rowwise(feed_weights.astype(bf16).T)

    integers = jnp.concatenate([tokens.reshape(-1), segments.reshape(-1), masked_pick.reshape(-1)])
    group = plane_gather_small(integers)

    def by_share(flat):
        return flat.reshape(n_seq, block, items).transpose(2, 0, 1).reshape(n_seq, count)

    size = block * items
    group_tokens = by_share(group[:, :size])
    own_segments = row_of(by_share(group[:, size : 2 * size]), seq_index)
    picks = group[:, 2 * size :].reshape(shares, n_seq // shares * slots)
    picks = row_of(picks, own_part)

    emb_low = embedding.astype(bf16)
    targets = jnp.asarray(keys) ^ seq_index
    wanted = by_distance(group_tokens, seq_index)[keys] - seq_index * vocab_rows

    def looked(table, ids):
        hot = ids[:, None] == jnp.arange(vocab_rows, dtype=jnp.int32)
        return dot(hot.astype(bf16), table).astype(bf16)

    def lookup():
        near = n_seq // 2
        _, (table, ids) = yield {}, (emb_low, wanted)
        odd = jnp.stack([looked(table, ids[near + k]) for k in range(near)])
        _, (table, ids, odd) = yield {}, (table, ids, odd)
        even = jnp.stack([looked(table, ids[k]) for k in range(near)])
        return (yield from plane_reduce(even, odd))

    def positions():
        near, far = yield from plane_gather(split_low(position_table))
        rows = jnp.concatenate([near, far]).reshape(n_seq, 2, block, width)
        rows = rows[:, 0].astype(f32) + rows[:, 1].astype(f32)
        blocks_here = n_seq // shares
        spots = np.argsort(keys).tolist()
        found = []
        for k in range(blocks_here):
            spot = chosen_of(spots, (own_part * blocks_here + k) ^ seq_index)
            found.append(lax.dynamic_index_in_dim(rows, spot, 0, keepdims=False))
        return jnp.concatenate(found)

    feed_all = [None] * n_dp

    def feed_spread():
        along = [feed_own]
        for _ in range(n_dp - 1):
            came, along = yield {along_dp: [along[-1]]}, along
            along = along + [came[along_dp][0]]
        along = jnp.stack(along)
        pieces = [
            lax.dynamic_index_in_dim(along, (place - places[m]) % n_dp, 0, keepdims=False)
            for m in range(n_dp)
        ]
        live, replies = {}, {}
        for number in range(2 * n_dp + n_seq):
            if number < n_dp:
                live[number] = plane_gather(pieces[number])
            sends, keeps, owners = {}, {}, {}
            for m, task in list(live.items()):
                try:
                    asked, keeps[m] = task.send(replies.get(m))
                except StopIteration as end:
                    feed_all[m] = end.value
                    del live[m]
                    continue
                for channel, parts in asked.items():
                    sends.setdefault(channel, []).extend(parts)
                    owners.setdefault(channel, []).extend([m] * len(parts))
            if not live:
                break
            came, (keeps, pieces) = yield sends, (keeps, pieces)
            replies = {m: ({}, kept) for m, kept in keeps.items()}
            for channel, names in owners.items():
                for m, part in zip(names, came[channel]):
                    replies[m][0].setdefault(channel, []).append(part)

    def aside():
        known = (picks, masked_labels, pair_labels)
        ids = [wanted + seq_index * vocab_rows]
        for step in range(n_dp - 1):
            came, (ids, known) = yield {along_dp: [ids[-1]]}, (ids, known)
            ids = ids + came[along_dp]
            if step == 0:
                known = from_integers(*known)
        return (ids, *known)

    def from_integers(picks, masked_labels, pair_labels):
        row_at = jnp.arange(n_seq // shares, dtype=jnp.int32)[:, None] * block + (
            picks.reshape(n_seq // shares, slots) // items
        )
        row_at = jnp.where(picks % items == own_item, row_at.reshape(-1), -1)
        labels = jnp.sum(jnp.where(jnp.arange(n_dp) == dp_index, masked_labels, 0), axis=1)
        label = row_of(pair_labels, own_item)
        masked_count = jnp.sum(masked_labels >= 0).astype(f32)
        return row_at, labels, label, masked_count

    def find_hits(ids):
        row_base = seq_index * vocab_rows + dp_index * quarter
        row_end = jnp.minimum(row_base + quarter, (seq_index + 1) * vocab_rows)
        ids = jnp.stack(ids)
        ids = jnp.where((ids >= row_base) & (ids < row_end), ids - row_base, -1)
        at = (targets % shares)[:, None] * count + jnp.arange(count, dtype=jnp.int32)
        at = at - seq_index * block
        at = jnp.where((at >= 0) & (at < block), at + quarter, -1)
        return ids.reshape(n_dp, 2, -1), at.reshape(2, -1)

    embedded, _, own_positions, integers_known = run(
        (0, lookup()),
        (0, feed_spread()),
        (0, positions()),
        (3, aside()),
    )
    all_ids, row_at, labels, label, masked_count = integers_known
    embedded = embedded + own_positions + jnp.where(own_segments[:, None] == 1, vectors[1], vectors[0])

    cos_hid, sin_hid = dft_constant(width)
    cos_hid, sin_hid = jnp.asarray(cos_hid), jnp.asarray(sin_hid)
    sources = own_part ^ jnp.arange(shares, dtype=jnp.int32)
    table_columns = (
        sources[:, None] * count + jnp.arange(count, dtype=jnp.int32)[None, :]
    ).reshape(-1)
    cos_seq, sin_seq = dft_rows(own_part * count, count, table_columns, length)

    bias_rel = by_distance(
        inner_bias.reshape(layers, n_seq, hidden // n_seq).swapaxes(0, 1), seq_index
    )[keys]
    bias_rel = bias_rel.swapaxes(0, 1).reshape(layers, 2, hidden // 2)

    def share_gather(value):
        held = value[None]
        for bit in bits_of(shares):
            held = jnp.concatenate([held, flip(held, bit)])
        return held

    def mix_forward(stream_low):
        pair = jnp.stack([dot(stream_low, cos_hid), dot(stream_low, sin_hid)]).astype(bf16)
        held = share_gather(pair)
        part_a = held[:, 0].reshape(length, width)
        part_b = held[:, 1].reshape(length, width)
        return lax.reduce_precision(dot(cos_seq, part_a) - dot(sin_seq, part_b), 8, 7)

    def mix_backward(grad_low):
        held = share_gather(grad_low).reshape(length, width)
        part_a = dot(cos_seq, held).astype(bf16)
        part_b = (-dot(sin_seq, held)).astype(bf16)
        return dot(part_a, cos_hid) + dot(part_b, sin_hid)

    unit_zero, scale_zero = norm_forward(embedded)
    stream = unit_zero * vectors[2] + vectors[2 + norms]
    saved = []
    for layer in range(layers):
        w_in, w_out = feed_all[2 * layer], feed_all[2 * layer + 1]
        gain_a, shift_a = vectors[3 + 2 * layer], vectors[3 + 2 * layer + norms]
        gain_b, shift_b = vectors[4 + 2 * layer], vectors[4 + 2 * layer + norms]
        mixed = mix_forward(stream.astype(bf16))
        unit_a, scale_a = norm_forward(stream + mixed)
        joined = unit_a * gain_a + shift_a
        joined_low = joined.astype(bf16)
        inner = [dot(joined_low, w_in[k], 1, 1) + bias_rel[layer, k] for k in range(2)]
        active_low = [gelu_tanh(part).astype(bf16) for part in inner]
        output = dot(active_low[0], w_out[0]) + dot(active_low[1], w_out[1])
        output = output + vectors[2 + 2 * norms + layer]
        unit_b, scale_b = norm_forward(joined + output)
        stream = unit_b * gain_b + shift_b
        saved.append((joined_low, inner, active_low, unit_a, scale_a, unit_b, scale_b))

    chosen = (row_at[:, None] == jnp.arange(count, dtype=jnp.int32)).astype(bf16)
    masked_part = items_sum(dot(chosen, stream.astype(bf16)).astype(bf16), shares)
    masked_rows = by_distance(share_gather(masked_part), own_part).reshape(n_seq * slots, width)

    pool_row = 2 + 2 * norms + layers
    leads = (own_part == 0).astype(f32)

    def pair_loss(first_row, pool_shift, class_rows):
        pooled = jnp.tanh(jnp.dot(first_row, pooler, precision=highest) + pool_shift)
        scores = jnp.sum(pooled * class_rows, axis=1)
        top_score = jnp.max(scores)
        log_sum = top_score + jnp.log(jnp.sum(jnp.exp(scores - top_score)))
        return log_sum - jnp.sum(jnp.where(jnp.arange(2) == label, scores, 0.0))

    first_row = stream[:1]
    pair_value, pair_back = jax.vjp(
        pair_loss, first_row, vectors[pool_row][None], vectors[pool_row + 1 : pool_row + 3]
    )
    d_first_row, d_pool_shift, d_class = pair_back(leads / all_items)

    logits = dot(masked_rows, emb_low, 1, 1) + head_bias
    vocab_ids = seq_index * vocab_rows + jnp.arange(vocab_rows, dtype=jnp.int32)
    is_target = labels[:, None] == vocab_ids[None, :]
    peak = jnp.max(logits, axis=1)
    totals = jnp.sum(jnp.exp(logits - peak[:, None]), axis=1)
    target = jnp.sum(jnp.where(is_target, logits, 0.0), axis=1)
    stats = plane_gather_small(jnp.stack([peak, totals, target]))
    peak_all = jnp.max(stats[:, 0], axis=0)
    log_total = peak_all + jnp.log(jnp.sum(stats[:, 1] * jnp.exp(stats[:, 0] - peak_all), axis=0))
    target_all = jnp.sum(stats[:, 2], axis=0)
    counted = labels >= 0
    leader = (seq_index == 0).astype(f32)
    masked_local = leader * jnp.sum(jnp.where(counted, log_total - target_all, 0.0))
    weighting = jnp.where(counted, 1.0 / masked_count, 0.0)
    d_logits = (jnp.exp(logits - log_total[:, None]) - is_target.astype(f32)) * weighting[:, None]
    d_head_bias = jnp.sum(d_logits, axis=0)
    d_logits_low = d_logits.astype(bf16)
    d_rows = dot(d_logits_low, emb_low).astype(bf16)
    d_rows = by_distance(d_rows.reshape(shares, n_seq // shares * slots, width), own_part)
    for bit in bits_of(shares)[::-1]:
        middle = d_rows.shape[0] // 2
        d_rows = add_low(d_rows[:middle], flip(d_rows[middle:], bit))
    d_rows = items_sum(d_rows[0], shares)
    d_stream = dot(chosen, d_rows, 0, 0)
    d_stream = d_stream.at[:1].add(d_first_row)

    extra = -(-quarter // (16 * width)) * 16
    d_embed_head = dot(d_logits_low, masked_rows, 0, 0).astype(bf16)
    d_embed_head = jnp.pad(d_embed_head, ((0, quarter * n_dp - vocab_rows), (0, 0)))
    bias_rows = jnp.pad(d_head_bias, (0, quarter * n_dp - vocab_rows)).reshape(n_dp, quarter)
    bias_rows = jnp.pad(bias_rows, ((0, 0), (0, extra * width - quarter)))
    d_embed_head = jnp.concatenate(
        [
            d_embed_head.reshape(n_dp, quarter, width),
            bias_rows.reshape(n_dp, extra, width).astype(bf16),
        ],
        axis=1,
    )

    layer_grads = [None] * layers
    feed_ready = {}
    box = {}

    def backward(d_stream):
        for layer in reversed(range(layers)):
            joined_low, inner, active_low, unit_a, scale_a, unit_b, scale_b = saved[layer]
            w_in, w_out = feed_all[2 * layer], feed_all[2 * layer + 1]
            d_second, d_gain_b, d_shift_b = norm_backward(
                d_stream, unit_b, scale_b, vectors[4 + 2 * layer]
            )
            d_bias_out = jnp.sum(d_second, axis=0)
            d_out_low = d_second.astype(bf16)
            d_w_out = [dot(part, d_out_low, 0, 0).astype(bf16) for part in active_low]
            d_joined, d_bias_in, d_w_in = d_second, [], []
            for k in range(2):
                d_active = dot(d_out_low, w_out[k], 1, 1)
                (d_inner,) = jax.vjp(gelu_tanh, inner[k])[1](d_active)
                d_bias_in.append(jnp.sum(d_inner, axis=0))
                d_in_low = d_inner.astype(bf16)
                d_w_in.append(dot(d_in_low, joined_low, 0, 0).astype(bf16))
                d_joined = d_joined + dot(d_in_low, w_in[k])
            _, (d_joined, d_w_in, d_w_out) = yield {}, (d_joined, d_w_in, d_w_out)
            feed_ready[2 * layer], feed_ready[2 * layer + 1] = d_w_in, d_w_out
            d_first, d_gain_a, d_shift_a = norm_backward(
                d_joined, unit_a, scale_a, vectors[3 + 2 * layer]
            )
            d_stream = d_first + mix_backward(d_first.astype(bf16))
            layer_grads[layer] = (
                jnp.concatenate(d_bias_in),
                d_bias_out,
                d_gain_a,
                d_shift_a,
                d_gain_b,
                d_shift_b,
            )
            _, d_stream = yield {}, d_stream
        box["stream"] = d_stream

    def later_reduce(layer):
        shape = (n_seq // 2, -1, width)
        even, odd = [
            jnp.concatenate(
                [feed_ready[2 * layer + m][side].reshape(shape) for m in range(2)], axis=1
            )
            for side in range(2)
        ]
        out = yield from plane_reduce(even, odd)
        middle = out.shape[0] // 2
        reduced[2 * layer], reduced[2 * layer + 1] = out[:middle], out[middle:]

    reduced = {}
    last = 2 * layers

    rows = jnp.arange(quarter + block, dtype=jnp.int32)
    def into(total, k, side, piece):
        ids, at = box["hits"][0][k, side], box["hits"][1][side]
        hot = (rows[:, None] == ids) | (rows[:, None] == at)
        part = dot(hot.astype(bf16), piece)
        return part if total is None else total + part

    def hits_known():
        _, ids = yield {}, all_ids
        _, box["hits"] = yield {}, find_hits(ids)

    def tokens_reduce():
        d_embedded, d_gain_zero, d_shift_zero = norm_backward(
            box["stream"], unit_zero, scale_zero, vectors[2]
        )
        box["gain"], box["shift"], box["embedded"] = d_gain_zero, d_shift_zero, d_embedded
        mine = d_embedded.astype(bf16)
        total = None
        if n_seq != 8:
            along = [mine]
            for k in range(n_dp):
                near, far = yield from plane_gather(along[-1])
                total = into(into(total, k, 0, near), k, 1, far)
                if k < n_dp - 1:
                    came, along = yield {along_dp: [along[-1]]}, along
                    along = along + [came[along_dp][0]]
            return total
        half = mine.shape[0] // 2
        plan = [
            {along_dp: 0, "first": 0},
            {along_dp: 1},
            {along_dp: 2, "first": 1, "second": 0},
            {"first": 2, "second": 1},
            {"first": 3, "second": 2},
            {"second": 3, "far": (0, 1)},
            {"far": (2, 3)},
        ]
        along, by_x, by_y, near, far = [mine], {}, {}, {}, {}
        ready = []
        for now in plan:
            sends = {}
            if along_dp in now:
                sends[along_dp] = [along[now[along_dp]]]
            if "first" in now:
                k = now["first"]
                sends[2], sends[4] = [along[k]], [along[k]]
            if "second" in now:
                k = now["second"]
                sends.setdefault(2, []).append(by_y[k][half:])
                sends.setdefault(4, []).append(by_x[k][:half])
            if "far" in now:
                sends[1] = [near[k] for k in now["far"]]
            for k, side in ready:
                total = into(total, k, side, (near, far)[side][k])
            ready = []
            came, kept = yield sends, (along, by_x, by_y, near, far, total)
            along, by_x, by_y, near, far, total = kept
            if along_dp in now:
                along = along + [came[along_dp][0]]
            if "first" in now:
                k = now["first"]
                by_x[k], by_y[k] = came[2][0], came[4][0]
            if "second" in now:
                k = now["second"]
                near[k] = jnp.concatenate([along[k], by_x[k], by_y[k], came[4][-1], came[2][-1]])
                ready.append((k, 0))
            if "far" in now:
                for k, part in zip(now["far"], came[1]):
                    far[k] = part
                    ready.append((k, 1))
        for k, side in ready:
            total = into(total, k, side, (near, far)[side][k])
        return total

    def feed_ring():
        stacked = jnp.stack([reduced[m].astype(bf16) for m in range(last)])
        return (yield from ring_reduce(stacked))

    def small_reduce():
        d_embedded = box["embedded"]
        is_second = (own_segments == 1)[:, None]
        d_type_zero = jnp.sum(jnp.where(is_second, 0.0, d_embedded), axis=0)
        d_type_one = jnp.sum(jnp.where(is_second, d_embedded, 0.0), axis=0)
        gain_rows, shift_rows = [box["gain"]], [box["shift"]]
        out_rows, inner_rows = [], []
        for layer in range(layers):
            d_bias_in, d_bias_out, d_gain_a, d_shift_a, d_gain_b, d_shift_b = layer_grads[layer]
            gain_rows += [d_gain_a, d_gain_b]
            shift_rows += [d_shift_a, d_shift_b]
            out_rows.append(d_bias_out)
            inner_rows.append(d_bias_in)
        d_vectors = jnp.stack(
            [d_type_zero, d_type_one]
            + gain_rows
            + shift_rows
            + out_rows
            + [d_pool_shift[0], d_class[0], d_class[1]]
        )
        spots = np.argsort(keys)
        d_inner = jnp.stack(inner_rows).reshape(layers, n_seq, hidden // n_seq).swapaxes(0, 1)
        d_inner = by_distance(d_inner[spots], seq_index).swapaxes(0, 1).reshape(layers, hidden)
        mine = (jnp.arange(all_items) == dp_index * items + own_item)[:, None] & (own_part == 0)
        small = jnp.concatenate(
            [
                d_vectors.reshape(-1),
                d_inner.reshape(-1),
                jnp.where(mine, first_row, 0.0).reshape(-1),
                jnp.where(mine, d_pool_shift, 0.0).reshape(-1),
                jnp.stack([masked_local, leads * pair_value]),
            ]
        )
        small = jnp.pad(small, (0, -small.shape[0] % (16 * width))).reshape(-1, width)
        return (yield from reduce_everywhere(small))

    rounds = 2 * layers
    plane_rounds = 3 if n_seq == 8 else len(bits_of(n_seq))
    feeds_done = rounds + plane_rounds
    out = run(
        (0, backward(d_stream)),
        (0, ring_reduce(d_embed_head, (0,) + (1,) * (n_dp - 2))),
        *[(2 * (layers - layer) - 1, later_reduce(layer)) for layer in reversed(range(layers))],
        (rounds - 1, hits_known()),
        (rounds, tokens_reduce()),
        (rounds + 1, small_reduce()),
        (feeds_done, feed_ring()),
    )
    d_embed_head, d_token, small, feed_grad = out[1], out[-3], out[-2], out[-1]
    feed_grad = rowwise(feed_grad).T
    d_embed_own = d_token[:quarter] + d_embed_head[:quarter]
    d_bias_own = d_embed_head[quarter:]
    d_position = d_token[quarter:]
    vector_count = vectors.shape[0]
    inner_count = layers * hidden // width
    d_vectors = small[:vector_count]
    d_inner = small[vector_count : vector_count + inner_count].reshape(layers, hidden)
    rest = small[vector_count + inner_count :]
    d_pooler = dot(rest[:all_items], rest[all_items : 2 * all_items], 0, 0, highest)
    masked_sum, pair_sum = rest[2 * all_items, 0], rest[2 * all_items, 1]

    dp_leader = (dp_index == 0).astype(f32)
    spread_squares = (
        jnp.sum(feed_grad * feed_grad)
        + jnp.sum(d_embed_own * d_embed_own)
        + jnp.sum(d_bias_own * d_bias_own)
        + dp_leader * jnp.sum(d_position * d_position)
    )
    small_squares = (
        jnp.sum(d_vectors * d_vectors) + jnp.sum(d_inner * d_inner) + jnp.sum(d_pooler * d_pooler)
    )
    spread_squares, small_squares = tie((spread_squares, small_squares))
    spread_squares = spread_squares.reshape(1, 1)
    for bit in bits_of(n_dp):
        spread_squares = spread_squares + flip(spread_squares, bit, "dp")
    d_embed_own, d_bias_own, spread_squares = tie((d_embed_own, d_bias_own, spread_squares))
    for bit in bits_of(n_seq):
        spread_squares = spread_squares + flip(spread_squares, bit)
    spread_squares = spread_squares[0, 0]
    grad_norm = jnp.sqrt(spread_squares + small_squares)
    clip = clip_limit / jnp.maximum(grad_norm, clip_limit)
    loss = masked_sum / masked_count + pair_sum / all_items

    own_quarter = jnp.concatenate([d_embed_own, d_bias_own]).astype(bf16)
    first_quarter = hop(own_quarter)

    moment = muon_keep * feed_moment + clip * feed_grad
    gram = square_sum(dot(moment, moment, 1, 1, high))
    scaling = 1.0 / (jnp.sqrt(jnp.trace(gram)) + 1e-07)
    gram = gram * (scaling * scaling)
    gram, first_quarter = tie((gram, first_quarter))
    second_quarter = hop(first_quarter)
    total, gram = sweeps(gram)
    total, gram, second_quarter = tie((total, gram, second_quarter))
    third_quarter = hop(second_quarter)
    total = sweeps(gram, total)
    ortho = dot(total, moment * scaling, 1, 0, high)
    quarters = jnp.stack([own_quarter, first_quarter, second_quarter, third_quarter])
    quarters = [
        lax.dynamic_index_in_dim(quarters, (place - places[k]) % n_dp, 0, keepdims=False)
        for k in range(n_dp)
    ]
    d_embed = jnp.concatenate([part[:quarter] for part in quarters])[:vocab_rows].astype(f32)
    d_head_bias = jnp.stack([part[quarter:].reshape(-1)[:quarter] for part in quarters])
    d_head_bias = d_head_bias.reshape(-1)[:vocab_rows].astype(f32)
    new_emb = adam_step(embedding, d_embed * clip, embed_first, embed_second, 0.02)
    new_pos = adam_step(position_table, d_position * clip, position_first, position_second, 0.01)
    new_head = adam_step(head_bias, d_head_bias * clip, head_first, head_second, 0.2)
    new_vec = adam_step(
        vectors, d_vectors * clip, vector_first, vector_second, vector_rates(layers)
    )
    new_inner = adam_step(inner_bias, d_inner * clip, inner_first, inner_second, 0.05)
    new_pool = adam_step(pooler, d_pooler * clip, pooler_first, pooler_second, 0.02)

    new_feed = (
        feed_weights * (1.0 - muon_rate * decay)
        - muon_rate * 0.2 * math.sqrt(max(width, hidden)) * ortho
    )
    return (
        loss,
        masked_count,
        grad_norm,
        new_emb[0],
        new_emb[1],
        new_emb[2],
        new_pos[0],
        new_pos[1],
        new_pos[2],
        new_head[0],
        new_head[1],
        new_head[2],
        new_vec[0],
        new_vec[1],
        new_vec[2],
        new_inner[0],
        new_inner[1],
        new_inner[2],
        new_pool[0],
        new_pool[1],
        new_pool[2],
        new_feed,
        moment,
    )


def solution(mesh):
    return jax.shard_map(
        shards,
        mesh=mesh,
        in_specs=(
            P("seq", "dp"),
            P("seq", "dp"),
            P("seq", "dp"),
            P(),
            P("dp"),
            P("seq", None),
            P("seq", None),
            P("seq", None),
            P("seq", None),
            P("seq", None),
            P("seq", None),
            P("seq"),
            P("seq"),
            P("seq"),
            P(),
            P(),
            P(),
            P(),
            P(),
            P(),
            P(),
            P(),
            P(),
            P(None, ("dp", "seq")),
            P(None, ("dp", "seq")),
        ),
        out_specs=(
            P(),
            P(),
            P(),
            P("seq", None),
            P("seq", None),
            P("seq", None),
            P("seq", None),
            P("seq", None),
            P("seq", None),
            P("seq"),
            P("seq"),
            P("seq"),
            P(),
            P(),
            P(),
            P(),
            P(),
            P(),
            P(),
            P(),
            P(),
            P(None, ("dp", "seq")),
            P(None, ("dp", "seq")),
        ),
        check_vma=False,
    )
```

```python
import functools
import math

import jax
import jax.numpy as jnp
import numpy as np
from jax import lax
from jax.experimental import pallas as pl
from jax.experimental.layout import Layout, with_layout_constraint
from jax.experimental.pallas import tpu as pltpu
from jax.sharding import PartitionSpec as P

STEP = 10

highest = lax.Precision.HIGHEST
high = lax.Precision.HIGH
f32 = jnp.float32
bf16 = jnp.bfloat16
norm_epsilon = 1e-06
beta_one = 0.5
beta_two = 0.5
adam_epsilon = 1e-08
decay = 0.01
clip_limit = 1.0
muon_rate = 0.05
muon_keep = 0.5
ns_first = 3.4445
ns_second = -4.775
ns_third = 2.0315


def quarters_kernel(rate, places_ref, clip_ref, one_ref, two_ref, weight_ref, first_ref, second_ref, *refs):
    new_weight_ref, new_first_ref, new_second_ref = refs[-3:]
    grad = jnp.where(pl.program_id(0) == 0, one_ref[...], two_ref[...]).astype(f32) * clip_ref[0, 0]
    new = adam_step(weight_ref[...], grad, first_ref[...], second_ref[...], rate)
    new_weight_ref[...], new_first_ref[...], new_second_ref[...] = new


def adam_quarters(rate, rows, places, clip, pieces, state, so_far=None):
    width = state[0].shape[1]
    block = max(k for k in range(16, 385, 16) if rows % k == 0)
    blocks = rows // block

    def spec(index):
        return pl.BlockSpec((block, width), index)

    own = spec(lambda c, b, places: (places[c] * blocks + b, 0))
    kept = [] if so_far is None else list(so_far)
    return pl.pallas_call(
        functools.partial(quarters_kernel, rate),
        out_shape=[jax.ShapeDtypeStruct(value.shape, value.dtype) for value in state],
        grid_spec=pltpu.PrefetchScalarGridSpec(
            num_scalar_prefetch=1,
            grid=(2, blocks),
            in_specs=[
                pl.BlockSpec(memory_space=pltpu.SMEM),
                spec(lambda c, b, places: (jnp.where(c == 0, b, blocks - 1), 0)),
                spec(lambda c, b, places: (jnp.where(c == 0, 0, b), 0)),
                own,
                own,
                own,
            ]
            + [pl.BlockSpec(memory_space=pl.ANY)] * len(kept),
            out_specs=[own, own, own],
        ),
        input_output_aliases={7 + k: k for k in range(len(kept))},
        compiler_params=pltpu.CompilerParams(vmem_limit_bytes=56 << 20),
        cost_estimate=pl.CostEstimate(
            flops=40 * rows * width, bytes_accessed=52 * rows * width, transcendentals=0
        ),
    )(jnp.stack(places).astype(jnp.int32), clip.reshape(1, 1), *pieces, *state, *kept)


def vector_rates(layers):
    rates = (
        [0.01, 0.01]
        + [0.2] * (2 * layers + 1)
        + [0.05] * (2 * layers + 1)
        + [0.05] * layers
        + [0.05, 0.02, 0.02]
    )
    return jnp.array(rates, f32)[:, None]


def tie(values):
    return lax.optimization_barrier(values)


def flip(value, bit, axis="seq"):
    return lax.ppermute(value, axis, [(k, k ^ bit) for k in range(lax.axis_size(axis))])


def bits_of(count):
    return [1 << k for k in range(count.bit_length() - 1)]


def ring_order(count):
    return [0] + list(range(1, count, 2)) + list(range(2, count, 2))[::-1]


def ring_place(count):
    order = ring_order(count)
    return [order.index(k) for k in range(count)]


def hop(value):
    count = lax.axis_size("dp")
    order = ring_order(count)
    return lax.ppermute(
        value, "dp", [(order[k], order[(k + 1) % count]) for k in range(count)]
    )


def ring_gather(value):
    out = [value]
    for _ in range(lax.axis_size("dp") - 1):
        out.append(hop(out[-1]))
    return out


def plane_keys(count):
    evens = list(range(0, count, 2))
    return evens + [k ^ 1 for k in evens]


def rowwise(value):
    return with_layout_constraint(value, Layout(tuple(range(value.ndim))))


along_dp = 0
few_rows = 384


def exchange(channel, value):
    return hop(value) if channel == along_dp else flip(value, channel)


def run(*tasks):
    results = [None] * len(tasks)
    live = dict(enumerate(tasks))
    replies = {}
    number = 0
    while live:
        sends, keeps = {}, {}
        for name, (first, task) in list(live.items()):
            if number < first:
                continue
            try:
                asked, keeps[name] = task.send(replies.get(name))
            except StopIteration as end:
                results[name] = end.value
                del live[name]
                continue
            for channel, parts in asked.items():
                sends.setdefault(channel, []).extend((name, part) for part in parts)
        came = {}
        for channel, parts in sends.items():
            few = [k for k, (_, part) in enumerate(parts) if part.shape[0] <= few_rows]
            came[channel] = {
                k: exchange(channel, part)
                for k, (_, part) in enumerate(parts)
                if k not in few or len(few) == 1
            }
            if len(few) > 1:
                came[channel]["few"] = exchange(
                    channel, jnp.concatenate([parts[k][1] for k in few])
                )
        came = [list(group.items()) for group in came.values()]
        labels = [[key for key, _ in group] for group in came]
        came = [[value for _, value in group] for group in came]
        came, keeps = tie((came, keeps)) if keeps else (came, keeps)
        came = {
            channel: dict(zip(names, group))
            for channel, names, group in zip(sends, labels, came)
        }
        replies = {name: ({}, kept) for name, kept in keeps.items()}
        for channel, parts in sends.items():
            start = 0
            for k, (name, part) in enumerate(parts):
                if k in came[channel]:
                    got = came[channel][k]
                else:
                    got = came[channel]["few"][start : start + part.shape[0]]
                    start += part.shape[0]
                replies[name][0].setdefault(channel, []).append(got)
        number += 1
    return results


def beside(*tasks):
    results = [None] * len(tasks)
    live = dict(enumerate(tasks))
    replies = {}
    while live:
        sends, keeps, counts = {}, {}, {}
        for name, task in list(live.items()):
            try:
                asked, keeps[name] = task.send(replies.get(name))
            except StopIteration as end:
                results[name] = end.value
                del live[name]
                continue
            for channel, parts in asked.items():
                sends.setdefault(channel, []).extend(parts)
                counts.setdefault(channel, []).extend([name] * len(parts))
        if not live:
            break
        came, keeps = yield sends, keeps
        replies = {name: ({}, kept) for name, kept in keeps.items()}
        for channel, names in counts.items():
            for name, part in zip(names, came[channel]):
                replies[name][0].setdefault(channel, []).append(part)
    return results


def plane_gather(piece):
    count = lax.axis_size("seq")
    if count == 8:
        half = piece.shape[0] // 2
        came, piece = yield {2: [piece], 4: [piece]}, piece
        by_x, by_y = came[2][0], came[4][0]
        came, kept = yield {4: [by_x[:half]], 2: [by_y[half:]]}, (piece, by_x, by_y)
        held = jnp.concatenate([*kept, came[4][0], came[2][0]])
    else:
        held = piece
        for bit in bits_of(count)[1:]:
            came, held = yield {bit: [held]}, held
            held = jnp.concatenate([held, came[bit][0]])
    return held, flip(held, 1)


def add_low(left, right):
    return (left.astype(f32) + right.astype(f32)).astype(bf16)


def chips_reduce(held):
    count = lax.axis_size("seq")
    if count == 8:
        half = held[0].shape[0] // 2
        came, held = yield {2: [held[3][:half]], 4: [held[3][half:]]}, held
        to_y = jnp.concatenate([add_low(held[2][:half], came[2][0]), held[2][half:]])
        to_x = jnp.concatenate([held[1][:half], add_low(held[1][half:], came[4][0])])
        came, mine = yield {2: [to_x], 4: [to_y]}, held[0]
        return mine.astype(f32) + came[2][0].astype(f32) + came[4][0].astype(f32)
    for bit in bits_of(count)[:0:-1]:
        middle = len(held) // 2
        came, held = yield {bit: held[middle:]}, held[:middle]
        held = [add_low(one, two) for one, two in zip(held, came[bit])]
    return held[0].astype(f32)


def plane_reduce(even, odd):
    came, even = yield {1: [odd.reshape(-1, odd.shape[-1])]}, even
    held = add_low(even, came[1][0].reshape(odd.shape))
    return (yield from chips_reduce([held[k] for k in range(held.shape[0])]))


def ring_reduce(values, waits=()):
    count = lax.axis_size("dp")
    index = lax.axis_index("dp")
    order = ring_order(count)
    place = chosen_of(ring_place(count), index)
    held = None
    for step in range(1, count):
        mine = lax.dynamic_index_in_dim(values, chosen_of(order, (place - step) % count), 0, keepdims=False)
        if held is not None:
            mine = add_low(mine, held)
        wait = waits[step - 1] if waits else 0
        if wait:
            held = hop(mine)
            for _ in range(wait):
                _, values = yield {}, values
            _, (values, held) = yield {}, (values, held)
        else:
            came, values = yield {along_dp: [mine]}, values
            held = came[along_dp][0]
    mine = lax.dynamic_index_in_dim(values, index, 0, keepdims=False)
    return mine.astype(f32) + held.astype(f32)


def split_low(value):
    top = lax.reduce_precision(value, 8, 7)
    return jnp.concatenate([top.astype(bf16), (value - top).astype(bf16)])


def join_low(value):
    middle = value.shape[0] // 2
    return value[:middle].astype(f32) + value[middle:].astype(f32)


def reduce_everywhere(value):
    for bit in bits_of(lax.axis_size("seq")):
        low = split_low(value)
        came, low = yield {bit: [low]}, low
        value = join_low(low) + join_low(came[bit][0])
    low = [split_low(value)]
    for _ in range(lax.axis_size("dp") - 1):
        came, low = yield {along_dp: [low[-1]]}, low
        low = low + [came[along_dp][0]]
    count = lax.axis_size("dp")
    places = ring_place(count)
    place = chosen_of(places, lax.axis_index("dp"))
    stacked = jnp.stack([join_low(part) for part in low])
    total = None
    for k in range(count):
        part = lax.dynamic_index_in_dim(stacked, (place - places[k]) % count, 0, keepdims=False)
        total = part if total is None else total + part
    return total


def square_sum(square):
    width = square.shape[0]
    part = width // 3
    pairs = [(0, 0), (0, 1), (0, 2), (1, 1), (1, 2), (2, 2)]
    blocks = [square[a * part : (a + 1) * part, b * part : (b + 1) * part] for a, b in pairs]
    held = jnp.concatenate(blocks)
    index = lax.axis_index("seq")

    def halve(value, bit):
        side = (index & bit) // bit
        middle = value.shape[0] // 2
        mine = lax.dynamic_slice_in_dim(value, side * middle, middle)
        other = lax.dynamic_slice_in_dim(value, (1 - side) * middle, middle)
        return mine + flip(other, bit)

    def join(value, bit):
        other = flip(value, bit)
        low = (index & bit) == 0
        return jnp.concatenate([jnp.where(low, value, other), jnp.where(low, other, value)])

    bits = bits_of(lax.axis_size("seq"))
    held = halve(held, 1)
    middle = held.shape[0] // 2
    one, two = held[:middle], held[middle:]
    for bit, other in zip(bits[1:], bits[:0:-1]):
        one, two = one + flip(one, bit), two + flip(two, other)
    held = jnp.concatenate([one, two])
    held = join(held, 1)
    found = {}
    for k, (a, b) in enumerate(pairs):
        block = held[k * part : (k + 1) * part]
        found[a, b] = block
        if a != b:
            found[b, a] = block.T
    return jnp.concatenate(
        [jnp.concatenate([found[a, b] for b in range(3)], axis=1) for a in range(3)]
    )


def items_sum(value, first_bit):
    bits = [b for b in bits_of(lax.axis_size("seq")) if b >= first_bit]
    half = value.shape[0] // 2
    top, bottom = value[:half], value[half:]
    for one, other in zip(bits, bits[::-1]):
        top, bottom = (
            add_low(top, flip(top, one)),
            add_low(bottom, flip(bottom, other)),
        )
    return jnp.concatenate([top, bottom])


def by_distance(values, index):
    count = values.shape[0]
    for bit in bits_of(count):
        pairs = values.reshape((count // (2 * bit), 2, bit) + values.shape[1:])
        swapped = jnp.concatenate([pairs[:, 1:], pairs[:, :1]], axis=1).reshape(values.shape)
        values = jnp.where(index & bit > 0, swapped, values)
    return values


def chosen_of(table, index):
    found = jnp.int32(table[0])
    for k, value in enumerate(table[1:], 1):
        found = jnp.where(index == k, jnp.int32(value), found)
    return found


def row_of(values, index):
    spots = jnp.arange(values.shape[0]).reshape((-1,) + (1,) * (values.ndim - 1))
    return jnp.sum(jnp.where(spots == index, values, 0), axis=0)


def plane_gather_small(value):
    held = value[None]
    for bit in bits_of(lax.axis_size("seq")):
        held = jnp.concatenate([held, flip(held, bit)])
    return by_distance(held, lax.axis_index("seq"))


def dft_constant(length):
    index = np.arange(length, dtype=np.int64)
    phase = (index[:, None] * index[None, :]) % length
    angle = phase.astype(np.float32) * np.float32(2.0 * math.pi / length)
    return np.cos(angle).astype(bf16), np.sin(angle).astype(bf16)


def dft_rows(first_row, row_total, columns, length):
    fine = 32 if row_total % 32 == 0 else 1

    def base(rows):
        phase = (rows[:, None] * columns[None, :]) % length
        angle = phase.astype(f32) * (2.0 * math.pi / length)
        return tie((jnp.cos(angle), jnp.sin(angle)))

    high_cos, high_sin = base(
        first_row + fine * jnp.arange(row_total // fine, dtype=jnp.int32)
    )
    low_cos, low_sin = base(jnp.arange(fine, dtype=jnp.int32))
    cosine = high_cos[:, None] * low_cos[None] - high_sin[:, None] * low_sin[None]
    sine = high_sin[:, None] * low_cos[None] + high_cos[:, None] * low_sin[None]
    shape = (row_total, columns.shape[0])
    return cosine.reshape(shape).astype(bf16), sine.reshape(shape).astype(bf16)


def norm_forward(values):
    centred = values - jnp.mean(values, axis=-1, keepdims=True)
    variance = jnp.mean(centred * centred, axis=-1, keepdims=True)
    scale = lax.rsqrt(variance + norm_epsilon)
    return centred * scale, scale


def norm_backward(grad, unit, scale, gain):
    inward = grad * gain
    average = jnp.mean(inward, axis=-1, keepdims=True)
    along = jnp.mean(inward * unit, axis=-1, keepdims=True)
    return (
        scale * (inward - average - unit * along),
        jnp.sum(grad * unit, axis=0),
        jnp.sum(grad, axis=0),
    )


def gelu_tanh(values):
    return jax.nn.gelu(values, approximate=True)


def dot(left, right, left_dim=1, right_dim=0, precision=None):
    return lax.dot_general(
        left,
        right,
        (((left_dim,), (right_dim,)), ((), ())),
        precision=precision,
        preferred_element_type=f32,
    )


def sweeps_kernel(part, coefficients, opening, *refs):
    if opening:
        gram_ref, out_ref, gram_s, poly_s, hold_s, left_s, right_s = refs
    else:
        gram_ref, so_far_ref, out_ref, gram_s, poly_s, hold_s, left_s, right_s = refs
    first, second, third = coefficients
    width = gram_ref.shape[0]
    blocks = width // part

    def pieces(value, count):
        out = []
        for _ in range(count):
            low = value.astype(jnp.bfloat16)
            out.append(low)
            value = value - low.astype(jnp.float32)
        return out

    def load(ref, side, source, terms):
        for row in range(blocks):
            rows = pl.ds(row * part, part)
            parts = pieces(source[rows, :], 1 + max(terms))
            for spot, term in enumerate(terms):
                if side == 0:
                    ref[rows, spot * width : (spot + 1) * width] = parts[term]
                else:
                    ref[pl.ds(spot * width + row * part, part), :] = parts[term]

    def product(target, more=False):
        for column in range(blocks):
            high = (column + 1) * part
            cols = slice(column * part, high)
            value = jnp.dot(
                left_s[:high, :], right_s[:, cols], preferred_element_type=jnp.float32
            )
            if more:
                value = value + target[:high, cols]
            target[:high, cols] = value
            for row in range(column):
                rows = slice(row * part, (row + 1) * part)
                target[cols, rows] = value[rows].T

    coarse = ((0, 1, 0), (0, 0, 1))
    rest = ((1, 0, 2), (1, 2, 0))

    def times(target, left, right, fine=False):
        load(left_s, 0, left, coarse[0])
        load(right_s, 1, right, coarse[1])
        product(target)
        if fine:
            load(left_s, 0, left, rest[0])
            load(right_s, 1, right, rest[1])
            product(target, True)

    def make_poly(fine=False):
        times(hold_s, gram_s, gram_s, fine)
        for row in range(blocks):
            rows = pl.ds(row * part, part)
            spot = lax.broadcasted_iota(jnp.int32, (part, width), 0) + row * part
            unit = spot == lax.broadcasted_iota(jnp.int32, (part, width), 1)
            poly_s[rows, :] = (
                jnp.where(unit, first, 0.0) + second * gram_s[rows, :] + third * hold_s[rows, :]
            )

    def next_gram(fine=False):
        times(hold_s, poly_s, gram_s, fine)
        times(gram_s, poly_s, hold_s, fine)

    def next_out():
        times(hold_s, poly_s, out_ref)
        out_ref[...] = hold_s[...]

    gram_s[...] = gram_ref[...]
    if opening:
        make_poly(True)
        out_ref[...] = poly_s[...]
        next_gram(True)
        make_poly()
        next_out()
        next_gram()
        return
    out_ref[...] = so_far_ref[...]

    @pl.loop(0, 2)
    def _(_):
        make_poly()
        next_out()
        next_gram()

    make_poly()
    next_out()


def sweeps(gram, so_far=None):
    width = gram.shape[0]
    opening = so_far is None
    square = jax.ShapeDtypeStruct((width, width), jnp.float32)
    scratch = pltpu.VMEM((width, width), jnp.float32)
    whole = pl.BlockSpec(memory_space=pltpu.VMEM)
    return pl.pallas_call(
        functools.partial(
            sweeps_kernel, width // 3, (ns_first, ns_second, ns_third), opening
        ),
        out_shape=[square, square] if opening else square,
        in_specs=[whole] if opening else [whole, whole],
        out_specs=[whole, whole] if opening else whole,
        scratch_shapes=([] if opening else [scratch])
        + [
            scratch,
            scratch,
            pltpu.VMEM((width, 3 * width), jnp.bfloat16),
            pltpu.VMEM((3 * width, width), jnp.bfloat16),
        ],
        compiler_params=pltpu.CompilerParams(vmem_limit_bytes=44 << 20),
        cost_estimate=pl.CostEstimate(
            flops=60 * width**3, bytes_accessed=16 * width * width, transcendentals=0
        ),
    )(*([gram] if opening else [gram, so_far]))


def adam_step(weight, grad, first, second, rate):
    first = beta_one * first + (1.0 - beta_one) * grad
    second = beta_two * second + (1.0 - beta_two) * grad * grad
    first_hat = first / (1.0 - beta_one**STEP)
    second_hat = second / (1.0 - beta_two**STEP)
    weight = weight - rate * (first_hat / (jnp.sqrt(second_hat) + adam_epsilon) + decay * weight)
    return (weight, first, second)


def shards(
    tokens,
    segments,
    masked_pick,
    masked_labels,
    pair_labels,
    embedding,
    embed_first,
    embed_second,
    position_table,
    position_first,
    position_second,
    head_bias,
    head_first,
    head_second,
    vectors,
    vector_first,
    vector_second,
    inner_bias,
    inner_first,
    inner_second,
    pooler,
    pooler_first,
    pooler_second,
    feed_weights,
    feed_moment,
):
    block, items = tokens.shape
    slots = masked_pick.shape[0]
    vocab_rows, width = embedding.shape
    layers, hidden = inner_bias.shape
    norms = 2 * layers + 1
    n_seq = lax.axis_size("seq")
    n_dp = lax.axis_size("dp")
    seq_index = lax.axis_index("seq")
    dp_index = lax.axis_index("dp")
    all_items = items * n_dp
    length = block * n_seq
    shares = n_seq // items
    count = length // shares
    own_item = seq_index // shares
    own_part = seq_index % shares
    keys = np.array(plane_keys(n_seq), np.int32)
    order = ring_order(n_dp)
    places = ring_place(n_dp)
    place = chosen_of(places, dp_index)
    quarter = -(-vocab_rows // (16 * n_dp)) * 16

    feed_own = rowwise(feed_weights.astype(bf16).T)

    integers = jnp.concatenate([tokens.reshape(-1), segments.reshape(-1), masked_pick.reshape(-1)])
    group = plane_gather_small(integers)

    def by_share(flat):
        return flat.reshape(n_seq, block, items).transpose(2, 0, 1).reshape(n_seq, count)

    size = block * items
    group_tokens = by_share(group[:, :size])
    own_segments = row_of(by_share(group[:, size : 2 * size]), seq_index)
    picks = group[:, 2 * size :].reshape(shares, n_seq // shares * slots)
    picks = row_of(picks, own_part)

    emb_low = embedding.astype(bf16)
    targets = jnp.asarray(keys) ^ seq_index
    wanted = by_distance(group_tokens, seq_index)[keys] - seq_index * vocab_rows

    def looked(table, ids):
        hot = ids[:, None] == jnp.arange(vocab_rows, dtype=jnp.int32)
        return dot(hot.astype(bf16), table).astype(bf16)

    def lookup():
        near = n_seq // 2
        _, (table, ids) = yield {}, (emb_low, wanted)
        odd = jnp.stack([looked(table, ids[near + k]) for k in range(near)])
        _, (table, ids, odd) = yield {}, (table, ids, odd)
        even = jnp.stack([looked(table, ids[k]) for k in range(near)])
        return (yield from plane_reduce(even, odd))

    def positions():
        near, far = yield from plane_gather(split_low(position_table))
        rows = jnp.concatenate([near, far]).reshape(n_seq, 2, block, width)
        rows = rows[:, 0].astype(f32) + rows[:, 1].astype(f32)
        blocks_here = n_seq // shares
        spots = np.argsort(keys).tolist()
        found = []
        for k in range(blocks_here):
            spot = chosen_of(spots, (own_part * blocks_here + k) ^ seq_index)
            found.append(lax.dynamic_index_in_dim(rows, spot, 0, keepdims=False))
        return jnp.concatenate(found)

    feed_all = [None] * n_dp

    def feed_spread():
        along = [feed_own]
        for _ in range(n_dp - 1):
            came, along = yield {along_dp: [along[-1]]}, along
            along = along + [came[along_dp][0]]
        along = jnp.stack(along)
        pieces = [
            lax.dynamic_index_in_dim(along, (place - places[m]) % n_dp, 0, keepdims=False)
            for m in range(n_dp)
        ]
        live, replies = {}, {}
        for number in range(2 * n_dp + n_seq):
            if number < n_dp:
                live[number] = plane_gather(pieces[number])
            sends, keeps, owners = {}, {}, {}
            for m, task in list(live.items()):
                try:
                    asked, keeps[m] = task.send(replies.get(m))
                except StopIteration as end:
                    feed_all[m] = end.value
                    del live[m]
                    continue
                for channel, parts in asked.items():
                    sends.setdefault(channel, []).extend(parts)
                    owners.setdefault(channel, []).extend([m] * len(parts))
            if not live:
                break
            came, (keeps, pieces) = yield sends, (keeps, pieces)
            replies = {m: ({}, kept) for m, kept in keeps.items()}
            for channel, names in owners.items():
                for m, part in zip(names, came[channel]):
                    replies[m][0].setdefault(channel, []).append(part)

    def aside():
        known = (picks, masked_labels, pair_labels)
        ids = [wanted + seq_index * vocab_rows]
        for step in range(n_dp - 1):
            came, (ids, known) = yield {along_dp: [ids[-1]]}, (ids, known)
            ids = ids + came[along_dp]
            if step == 0:
                known = from_integers(*known)
        return (ids, *known)

    def from_integers(picks, masked_labels, pair_labels):
        row_at = jnp.arange(n_seq // shares, dtype=jnp.int32)[:, None] * block + (
            picks.reshape(n_seq // shares, slots) // items
        )
        row_at = jnp.where(picks % items == own_item, row_at.reshape(-1), -1)
        labels = jnp.sum(jnp.where(jnp.arange(n_dp) == dp_index, masked_labels, 0), axis=1)
        label = row_of(pair_labels, own_item)
        masked_count = jnp.sum(masked_labels >= 0).astype(f32)
        return row_at, labels, label, masked_count

    def find_hits(ids):
        row_base = seq_index * vocab_rows + dp_index * quarter
        row_end = jnp.minimum(row_base + quarter, (seq_index + 1) * vocab_rows)
        ids = jnp.stack(ids)
        ids = jnp.where((ids >= row_base) & (ids < row_end), ids - row_base, -1)
        at = (targets % shares)[:, None] * count + jnp.arange(count, dtype=jnp.int32)
        at = at - seq_index * block
        at = jnp.where((at >= 0) & (at < block), at + quarter, -1)
        return ids.reshape(n_dp, 2, -1), at.reshape(2, -1)

    embedded, _, own_positions, integers_known = run(
        (0, lookup()),
        (0, feed_spread()),
        (0, positions()),
        (3, aside()),
    )
    all_ids, row_at, labels, label, masked_count = integers_known
    embedded = embedded + own_positions + jnp.where(own_segments[:, None] == 1, vectors[1], vectors[0])

    cos_hid, sin_hid = dft_constant(width)
    cos_hid, sin_hid = jnp.asarray(cos_hid), jnp.asarray(sin_hid)
    sources = own_part ^ jnp.arange(shares, dtype=jnp.int32)
    table_columns = (
        sources[:, None] * count + jnp.arange(count, dtype=jnp.int32)[None, :]
    ).reshape(-1)
    cos_seq, sin_seq = dft_rows(own_part * count, count, table_columns, length)

    bias_rel = by_distance(
        inner_bias.reshape(layers, n_seq, hidden // n_seq).swapaxes(0, 1), seq_index
    )[keys]
    bias_rel = bias_rel.swapaxes(0, 1).reshape(layers, 2, hidden // 2)

    def share_gather(value):
        held = value[None]
        for bit in bits_of(shares):
            held = jnp.concatenate([held, flip(held, bit)])
        return held

    def mix_forward(stream_low):
        pair = jnp.stack([dot(stream_low, cos_hid), dot(stream_low, sin_hid)]).astype(bf16)
        held = share_gather(pair)
        part_a = held[:, 0].reshape(length, width)
        part_b = held[:, 1].reshape(length, width)
        return lax.reduce_precision(dot(cos_seq, part_a) - dot(sin_seq, part_b), 8, 7)

    def mix_backward(grad_low):
        held = share_gather(grad_low).reshape(length, width)
        part_a = dot(cos_seq, held).astype(bf16)
        part_b = (-dot(sin_seq, held)).astype(bf16)
        return dot(part_a, cos_hid) + dot(part_b, sin_hid)

    unit_zero, scale_zero = norm_forward(embedded)
    stream = unit_zero * vectors[2] + vectors[2 + norms]
    saved = []
    for layer in range(layers):
        w_in, w_out = feed_all[2 * layer], feed_all[2 * layer + 1]
        gain_a, shift_a = vectors[3 + 2 * layer], vectors[3 + 2 * layer + norms]
        gain_b, shift_b = vectors[4 + 2 * layer], vectors[4 + 2 * layer + norms]
        mixed = mix_forward(stream.astype(bf16))
        unit_a, scale_a = norm_forward(stream + mixed)
        joined = unit_a * gain_a + shift_a
        joined_low = joined.astype(bf16)
        inner = [dot(joined_low, w_in[k], 1, 1) + bias_rel[layer, k] for k in range(2)]
        active_low = [gelu_tanh(part).astype(bf16) for part in inner]
        output = dot(active_low[0], w_out[0]) + dot(active_low[1], w_out[1])
        output = output + vectors[2 + 2 * norms + layer]
        unit_b, scale_b = norm_forward(joined + output)
        stream = unit_b * gain_b + shift_b
        saved.append((joined_low, inner, active_low, unit_a, scale_a, unit_b, scale_b))

    chosen = (row_at[:, None] == jnp.arange(count, dtype=jnp.int32)).astype(bf16)
    masked_part = items_sum(dot(chosen, stream.astype(bf16)).astype(bf16), shares)
    masked_rows = by_distance(share_gather(masked_part), own_part).reshape(n_seq * slots, width)

    pool_row = 2 + 2 * norms + layers
    leads = (own_part == 0).astype(f32)

    def pair_loss(first_row, pool_shift, class_rows):
        pooled = jnp.tanh(jnp.dot(first_row, pooler, precision=highest) + pool_shift)
        scores = jnp.sum(pooled * class_rows, axis=1)
        top_score = jnp.max(scores)
        log_sum = top_score + jnp.log(jnp.sum(jnp.exp(scores - top_score)))
        return log_sum - jnp.sum(jnp.where(jnp.arange(2) == label, scores, 0.0))

    first_row = stream[:1]
    pair_value, pair_back = jax.vjp(
        pair_loss, first_row, vectors[pool_row][None], vectors[pool_row + 1 : pool_row + 3]
    )
    d_first_row, d_pool_shift, d_class = pair_back(leads / all_items)

    logits = dot(masked_rows, emb_low, 1, 1) + head_bias
    vocab_ids = seq_index * vocab_rows + jnp.arange(vocab_rows, dtype=jnp.int32)
    is_target = labels[:, None] == vocab_ids[None, :]
    peak = jnp.max(logits, axis=1)
    totals = jnp.sum(jnp.exp(logits - peak[:, None]), axis=1)
    target = jnp.sum(jnp.where(is_target, logits, 0.0), axis=1)
    stats = plane_gather_small(jnp.stack([peak, totals, target]))
    peak_all = jnp.max(stats[:, 0], axis=0)
    log_total = peak_all + jnp.log(jnp.sum(stats[:, 1] * jnp.exp(stats[:, 0] - peak_all), axis=0))
    target_all = jnp.sum(stats[:, 2], axis=0)
    counted = labels >= 0
    leader = (seq_index == 0).astype(f32)
    masked_local = leader * jnp.sum(jnp.where(counted, log_total - target_all, 0.0))
    weighting = jnp.where(counted, 1.0 / masked_count, 0.0)
    d_logits = (jnp.exp(logits - log_total[:, None]) - is_target.astype(f32)) * weighting[:, None]
    d_head_bias = jnp.sum(d_logits, axis=0)
    d_logits_low = d_logits.astype(bf16)
    d_rows = dot(d_logits_low, emb_low).astype(bf16)
    d_rows = by_distance(d_rows.reshape(shares, n_seq // shares * slots, width), own_part)
    for bit in bits_of(shares)[::-1]:
        middle = d_rows.shape[0] // 2
        d_rows = add_low(d_rows[:middle], flip(d_rows[middle:], bit))
    d_rows = items_sum(d_rows[0], shares)
    d_stream = dot(chosen, d_rows, 0, 0)
    d_stream = d_stream.at[:1].add(d_first_row)

    extra = -(-quarter // (16 * width)) * 16
    d_embed_head = dot(d_logits_low, masked_rows, 0, 0).astype(bf16)
    d_embed_head = jnp.pad(d_embed_head, ((0, quarter * n_dp - vocab_rows), (0, 0)))
    bias_rows = jnp.pad(d_head_bias, (0, quarter * n_dp - vocab_rows)).reshape(n_dp, quarter)
    bias_rows = jnp.pad(bias_rows, ((0, 0), (0, extra * width - quarter)))
    d_embed_head = jnp.concatenate(
        [
            d_embed_head.reshape(n_dp, quarter, width),
            bias_rows.reshape(n_dp, extra, width).astype(bf16),
        ],
        axis=1,
    )

    layer_grads = [None] * layers
    feed_ready = {}
    box = {}

    def backward(d_stream):
        for layer in reversed(range(layers)):
            joined_low, inner, active_low, unit_a, scale_a, unit_b, scale_b = saved[layer]
            w_in, w_out = feed_all[2 * layer], feed_all[2 * layer + 1]
            d_second, d_gain_b, d_shift_b = norm_backward(
                d_stream, unit_b, scale_b, vectors[4 + 2 * layer]
            )
            d_bias_out = jnp.sum(d_second, axis=0)
            d_out_low = d_second.astype(bf16)
            d_w_out = [dot(part, d_out_low, 0, 0).astype(bf16) for part in active_low]
            d_joined, d_bias_in, d_w_in = d_second, [], []
            for k in range(2):
                d_active = dot(d_out_low, w_out[k], 1, 1)
                (d_inner,) = jax.vjp(gelu_tanh, inner[k])[1](d_active)
                d_bias_in.append(jnp.sum(d_inner, axis=0))
                d_in_low = d_inner.astype(bf16)
                d_w_in.append(dot(d_in_low, joined_low, 0, 0).astype(bf16))
                d_joined = d_joined + dot(d_in_low, w_in[k])
            _, (d_joined, d_w_in, d_w_out) = yield {}, (d_joined, d_w_in, d_w_out)
            feed_ready[2 * layer], feed_ready[2 * layer + 1] = d_w_in, d_w_out
            d_first, d_gain_a, d_shift_a = norm_backward(
                d_joined, unit_a, scale_a, vectors[3 + 2 * layer]
            )
            d_stream = d_first + mix_backward(d_first.astype(bf16))
            layer_grads[layer] = (
                jnp.concatenate(d_bias_in),
                d_bias_out,
                d_gain_a,
                d_shift_a,
                d_gain_b,
                d_shift_b,
            )
            _, d_stream = yield {}, d_stream
        box["stream"] = d_stream

    def later_reduce(layer):
        shape = (n_seq // 2, -1, width)
        even, odd = [
            jnp.concatenate(
                [feed_ready[2 * layer + m][side].reshape(shape) for m in range(2)], axis=1
            )
            for side in range(2)
        ]
        out = yield from plane_reduce(even, odd)
        middle = out.shape[0] // 2
        reduced[2 * layer], reduced[2 * layer + 1] = out[:middle], out[middle:]

    reduced = {}
    last = 2 * layers

    rows = jnp.arange(quarter + block, dtype=jnp.int32)
    def into(total, k, side, piece):
        ids, at = box["hits"][0][k, side], box["hits"][1][side]
        hot = (rows[:, None] == ids) | (rows[:, None] == at)
        part = dot(hot.astype(bf16), piece)
        return part if total is None else total + part

    def hits_known():
        _, ids = yield {}, all_ids
        _, box["hits"] = yield {}, find_hits(ids)

    def tokens_reduce():
        d_embedded, d_gain_zero, d_shift_zero = norm_backward(
            box["stream"], unit_zero, scale_zero, vectors[2]
        )
        box["gain"], box["shift"], box["embedded"] = d_gain_zero, d_shift_zero, d_embedded
        mine = d_embedded.astype(bf16)
        total = None
        if n_seq != 8:
            along = [mine]
            for k in range(n_dp):
                near, far = yield from plane_gather(along[-1])
                total = into(into(total, k, 0, near), k, 1, far)
                if k < n_dp - 1:
                    came, along = yield {along_dp: [along[-1]]}, along
                    along = along + [came[along_dp][0]]
            return total
        half = mine.shape[0] // 2
        plan = [
            {along_dp: 0, "first": 0},
            {along_dp: 1},
            {along_dp: 2, "first": 1, "second": 0},
            {"first": 2, "second": 1},
            {"first": 3, "second": 2},
            {"second": 3, "far": (0, 1)},
            {"far": (2, 3)},
        ]
        along, by_x, by_y, near, far = [mine], {}, {}, {}, {}
        ready = []
        for now in plan:
            sends = {}
            if along_dp in now:
                sends[along_dp] = [along[now[along_dp]]]
            if "first" in now:
                k = now["first"]
                sends[2], sends[4] = [along[k]], [along[k]]
            if "second" in now:
                k = now["second"]
                sends.setdefault(2, []).append(by_y[k][half:])
                sends.setdefault(4, []).append(by_x[k][:half])
            if "far" in now:
                sends[1] = [near[k] for k in now["far"]]
            for k, side in ready:
                total = into(total, k, side, (near, far)[side][k])
            ready = []
            came, kept = yield sends, (along, by_x, by_y, near, far, total)
            along, by_x, by_y, near, far, total = kept
            if along_dp in now:
                along = along + [came[along_dp][0]]
            if "first" in now:
                k = now["first"]
                by_x[k], by_y[k] = came[2][0], came[4][0]
            if "second" in now:
                k = now["second"]
                near[k] = jnp.concatenate([along[k], by_x[k], by_y[k], came[4][-1], came[2][-1]])
                ready.append((k, 0))
            if "far" in now:
                for k, part in zip(now["far"], came[1]):
                    far[k] = part
                    ready.append((k, 1))
        for k, side in ready:
            total = into(total, k, side, (near, far)[side][k])
        return total

    def feed_ring():
        stacked = jnp.stack([reduced[m].astype(bf16) for m in range(last)])
        return (yield from ring_reduce(stacked))

    def small_reduce():
        d_embedded = box["embedded"]
        is_second = (own_segments == 1)[:, None]
        d_type_zero = jnp.sum(jnp.where(is_second, 0.0, d_embedded), axis=0)
        d_type_one = jnp.sum(jnp.where(is_second, d_embedded, 0.0), axis=0)
        gain_rows, shift_rows = [box["gain"]], [box["shift"]]
        out_rows, inner_rows = [], []
        for layer in range(layers):
            d_bias_in, d_bias_out, d_gain_a, d_shift_a, d_gain_b, d_shift_b = layer_grads[layer]
            gain_rows += [d_gain_a, d_gain_b]
            shift_rows += [d_shift_a, d_shift_b]
            out_rows.append(d_bias_out)
            inner_rows.append(d_bias_in)
        d_vectors = jnp.stack(
            [d_type_zero, d_type_one]
            + gain_rows
            + shift_rows
            + out_rows
            + [d_pool_shift[0], d_class[0], d_class[1]]
        )
        spots = np.argsort(keys)
        d_inner = jnp.stack(inner_rows).reshape(layers, n_seq, hidden // n_seq).swapaxes(0, 1)
        d_inner = by_distance(d_inner[spots], seq_index).swapaxes(0, 1).reshape(layers, hidden)
        mine = (jnp.arange(all_items) == dp_index * items + own_item)[:, None] & (own_part == 0)
        small = jnp.concatenate(
            [
                d_vectors.reshape(-1),
                d_inner.reshape(-1),
                jnp.where(mine, first_row, 0.0).reshape(-1),
                jnp.where(mine, d_pool_shift, 0.0).reshape(-1),
                jnp.stack([masked_local, leads * pair_value]),
            ]
        )
        small = jnp.pad(small, (0, -small.shape[0] % (16 * width))).reshape(-1, width)
        return (yield from reduce_everywhere(small))

    rounds = 2 * layers
    plane_rounds = 3 if n_seq == 8 else len(bits_of(n_seq))
    feeds_done = rounds + plane_rounds
    out = run(
        (0, backward(d_stream)),
        (0, ring_reduce(d_embed_head, (0,) + (1,) * (n_dp - 2))),
        *[(2 * (layers - layer) - 1, later_reduce(layer)) for layer in reversed(range(layers))],
        (rounds - 1, hits_known()),
        (rounds, tokens_reduce()),
        (rounds + 1, small_reduce()),
        (feeds_done, feed_ring()),
    )
    d_embed_head, d_token, small, feed_grad = out[1], out[-3], out[-2], out[-1]
    feed_grad = rowwise(feed_grad).T
    d_embed_own = d_token[:quarter] + d_embed_head[:quarter]
    d_bias_own = d_embed_head[quarter:]
    d_position = d_token[quarter:]
    vector_count = vectors.shape[0]
    inner_count = layers * hidden // width
    d_vectors = small[:vector_count]
    d_inner = small[vector_count : vector_count + inner_count].reshape(layers, hidden)
    rest = small[vector_count + inner_count :]
    d_pooler = dot(rest[:all_items], rest[all_items : 2 * all_items], 0, 0, highest)
    masked_sum, pair_sum = rest[2 * all_items, 0], rest[2 * all_items, 1]

    dp_leader = (dp_index == 0).astype(f32)
    spread_squares = (
        jnp.sum(feed_grad * feed_grad)
        + jnp.sum(d_embed_own * d_embed_own)
        + jnp.sum(d_bias_own * d_bias_own)
        + dp_leader * jnp.sum(d_position * d_position)
    )
    small_squares = (
        jnp.sum(d_vectors * d_vectors) + jnp.sum(d_inner * d_inner) + jnp.sum(d_pooler * d_pooler)
    )
    spread_squares, small_squares = tie((spread_squares, small_squares))
    spread_squares = spread_squares.reshape(1, 1)
    for bit in bits_of(n_dp):
        spread_squares = spread_squares + flip(spread_squares, bit, "dp")
    d_embed_own, d_bias_own, spread_squares = tie((d_embed_own, d_bias_own, spread_squares))
    for bit in bits_of(n_seq):
        spread_squares = spread_squares + flip(spread_squares, bit)
    spread_squares = spread_squares[0, 0]
    grad_norm = jnp.sqrt(spread_squares + small_squares)
    clip = clip_limit / jnp.maximum(grad_norm, clip_limit)
    loss = masked_sum / masked_count + pair_sum / all_items

    own_quarter = jnp.concatenate([d_embed_own, d_bias_own]).astype(bf16)
    first_quarter = hop(own_quarter)

    moment = muon_keep * feed_moment + clip * feed_grad
    gram = square_sum(dot(moment, moment, 1, 1, high))
    scaling = 1.0 / (jnp.sqrt(jnp.trace(gram)) + 1e-07)
    gram = gram * (scaling * scaling)
    gram, first_quarter = tie((gram, first_quarter))
    second_quarter = hop(first_quarter)
    total, gram = sweeps(gram)
    total, gram, second_quarter = tie((total, gram, second_quarter))
    third_quarter = hop(second_quarter)
    total = sweeps(gram, total)
    total, own_quarter, first_quarter = tie((total, own_quarter, first_quarter))
    ortho = dot(total, moment * scaling, 1, 0, high)
    state = (embedding, embed_first, embed_second)
    near_places = [chosen_of(order, (place - k) % n_dp) for k in range(n_dp)]
    new_emb = adam_quarters(
        0.02, quarter, near_places[:2], clip, (own_quarter, first_quarter), state
    )
    new_emb, third_quarter, ortho = tie((new_emb, third_quarter, ortho))
    new_emb = adam_quarters(
        0.02, quarter, near_places[2:], clip, (second_quarter, third_quarter), state, new_emb
    )
    biases = [part[quarter:] for part in (own_quarter, first_quarter, second_quarter, third_quarter)]
    biases = jnp.stack(biases).reshape(n_dp, -1)[:, :quarter].astype(f32)
    d_head_bias = [
        lax.dynamic_index_in_dim(biases, (place - places[k]) % n_dp, 0, keepdims=False)
        for k in range(n_dp)
    ]
    d_head_bias = jnp.concatenate(d_head_bias)[:vocab_rows]
    new_pos = adam_step(position_table, d_position * clip, position_first, position_second, 0.01)
    new_head = adam_step(head_bias, d_head_bias * clip, head_first, head_second, 0.2)
    new_vec = adam_step(
        vectors, d_vectors * clip, vector_first, vector_second, vector_rates(layers)
    )
    new_inner = adam_step(inner_bias, d_inner * clip, inner_first, inner_second, 0.05)
    new_pool = adam_step(pooler, d_pooler * clip, pooler_first, pooler_second, 0.02)

    new_feed = (
        feed_weights * (1.0 - muon_rate * decay)
        - muon_rate * 0.2 * math.sqrt(max(width, hidden)) * ortho
    )
    return (
        loss,
        masked_count,
        grad_norm,
        new_emb[0],
        new_emb[1],
        new_emb[2],
        new_pos[0],
        new_pos[1],
        new_pos[2],
        new_head[0],
        new_head[1],
        new_head[2],
        new_vec[0],
        new_vec[1],
        new_vec[2],
        new_inner[0],
        new_inner[1],
        new_inner[2],
        new_pool[0],
        new_pool[1],
        new_pool[2],
        new_feed,
        moment,
    )


def solution(mesh):
    return jax.shard_map(
        shards,
        mesh=mesh,
        in_specs=(
            P("seq", "dp"),
            P("seq", "dp"),
            P("seq", "dp"),
            P(),
            P("dp"),
            P("seq", None),
            P("seq", None),
            P("seq", None),
            P("seq", None),
            P("seq", None),
            P("seq", None),
            P("seq"),
            P("seq"),
            P("seq"),
            P(),
            P(),
            P(),
            P(),
            P(),
            P(),
            P(),
            P(),
            P(),
            P(None, ("dp", "seq")),
            P(None, ("dp", "seq")),
        ),
        out_specs=(
            P(),
            P(),
            P(),
            P("seq", None),
            P("seq", None),
            P("seq", None),
            P("seq", None),
            P("seq", None),
            P("seq", None),
            P("seq"),
            P("seq"),
            P("seq"),
            P(),
            P(),
            P(),
            P(),
            P(),
            P(),
            P(),
            P(),
            P(),
            P(None, ("dp", "seq")),
            P(None, ("dp", "seq")),
        ),
        check_vma=False,
    )
```
